512 devices in a mesh: ia: 8 (over y, core), ja: 8 (over z_lo), al: 8 (over z_hi, x).
Axes of the slice: x: 4, y: 4, z: 16 (z_hi: 2, z_lo: 8; z = z_hi * 8 + z_lo), core: 2. Of those that a mesh axis runs over, the one named last changes fastest.
Arguments:
- text_states: bfloat16 [2048, 8192], P(('ja', 'ia'), 'al'), may hold values from -6 to 6
- latents: bfloat16 [256, 8192], P(('ja', 'ia'), 'al'), may hold values from -6 to 6
- w_query: bfloat16 [8192, 4096], P(('al', 'ja'), 'ia'), may hold values from -0.0625 to 0.0625
- w_key: bfloat16 [8192, 4096], P(('al', 'ja'), 'ia'), may hold values from -0.0625 to 0.0625
- w_value: bfloat16 [8192, 4096], P(('al', 'ja'), 'ia'), may hold values from -0.0625 to 0.0625
- w_output: bfloat16 [4096, 8192], P('ia', ('al', 'ja')), may hold values from -0.09375 to 0.09375
- gate_logit: float32 [8192], P('al'), may hold values from 0.3 to 1.6
- image_index: int32 [2048], P(('ja', 'al')), may hold values from 0 to 3, as said below
- latent_count: int32 [4], replicated, may hold values from 1 to 64, as said below
- grad_output: bfloat16 [2048, 8192], P(('ja', 'ia'), 'al'), may hold values from -6 to 6
Outputs:
- mixed: bfloat16 [2048, 8192], P(('ja', 'ia'), 'al')
- grad_states: bfloat16 [2048, 8192], P(('ja', 'ia'), 'al')
- grad_latents: bfloat16 [256, 8192], P(('ja', 'ia'), 'al')
- grad_w_query: float32 [8192, 4096], P(('al', 'ja'), 'ia')
- grad_w_key: float32 [8192, 4096], P(('al', 'ja'), 'ia')
- grad_w_value: float32 [8192, 4096], P(('al', 'ja'), 'ia')
- grad_w_output: float32 [4096, 8192], P('ia', ('al', 'ja'))
- grad_gate: float32 [8192], P('al')
The draws below stay inside these ranges and needn't reach their ends.
Inputs may be any that keep to these rules, and one draw needn't show every extreme that they name: `image_index`: image indices never fall along the tokens; token 0 attends image 0 and the last token the last image. `latent_count`: some image has all 64 latents live.
All inputs are finite; a program needn't handle non-finite values.
Results may differ from the reference program's by a relative error of at most 0.035.
Values may be sent and summed in bfloat16 or wider, within the bound.
A program may use at most 64 MiB of HBM per device.

```python
import math
import jax
import jax.numpy as jnp
from jax import lax

D = 8192
HEADS = 32
HS = 128
LAT = 64
IMGS = 4
HD = 4096
NL = 256
TOKENS = 2048
N_IA = 8
N_JA = 8
N_AL = 8


def draw_image_index(key, part):
    key = jax.random.fold_in(key, 11)
    cuts = jnp.sort(jax.random.randint(key, (IMGS - 1,), 1, TOKENS))
    positions = jnp.arange(TOKENS, dtype=jnp.int32)
    return jnp.sum((positions[:, None] >= cuts[None, :]).astype(jnp.int32), axis=1).astype(jnp.int32)


def draw_latent_count(key, part):
    key = jax.random.fold_in(key, 23)
    first_key, second_key = jax.random.split(key)
    counts = jax.random.randint(first_key, (IMGS,), 1, LAT + 1)
    chosen = jax.random.randint(second_key, (), 0, IMGS)
    return jnp.where(jnp.arange(IMGS, dtype=jnp.int32) == chosen, LAT, counts).astype(jnp.int32)


def level_of(rng, extent, cuts, least, high):
    level, own = 1.0, jax.random.fold_in(rng, 6)
    for position, shards_of in cuts:
        heights = jnp.exp(jax.random.uniform(jax.random.fold_in(own, position), (shards_of,), jnp.float32, least / len(cuts), high / len(cuts)))
        level = level * jnp.repeat(heights, extent[position] // shards_of).reshape([-1 if axis == position else 1 for axis in range(len(extent))])
    return level


def noise(own_key, dims, spread, limit, cuts=(), held_as=jnp.bfloat16):
    result = jax.random.normal(own_key, dims, jnp.float32) * spread
    if len(cuts) > 0:
        result = level_of(own_key, dims, cuts, -0.22, 0.18) * result
    return jnp.clip(result, min=-limit, max=limit).astype(held_as)


def setup_inputs(seed: int = 0) -> dict:
    streams_of = jax.random.split(jax.random.key(seed), 11)
    text_states = noise(streams_of[0], (TOKENS, D), 1.0, 6.0, ((0, 64), (1, 8)))
    latents = noise(streams_of[1], (NL, D), 1.0, 6.0, ((0, 64), (1, 8)))
    w_query = noise(streams_of[2], (D, HD), D ** -0.5, 0.0625, ((0, 64), (1, 8)))
    w_key = noise(streams_of[3], (D, HD), D ** -0.5, 0.0625, ((0, 64), (1, 8)))
    w_value = noise(streams_of[4], (D, HD), D ** -0.5, 0.0625, ((0, 64), (1, 8)))
    w_output = noise(streams_of[5], (HD, D), HD ** -0.5, 0.09375, ((0, 8), (1, 64)))
    gate_logit = jnp.clip(0.3 + 1.3 * jax.random.uniform(streams_of[6], (D,), jnp.float32) ** level_of(streams_of[6], (D,), ((0, 8),), -0.2, 0.2), 0.3, 1.6)
    image_index = draw_image_index(jax.random.fold_in(streams_of[10], 71), 0)
    latent_count = draw_latent_count(jax.random.fold_in(streams_of[10], 71), 0)
    grad_output = noise(streams_of[9], (TOKENS, D), 1.0, 6.0, ((0, 64), (1, 8)))
    return dict(text_states=text_states, latents=latents, w_query=w_query, w_key=w_key, w_value=w_value, w_output=w_output, gate_logit=gate_logit, image_index=image_index, latent_count=latent_count, grad_output=grad_output)


EPS = 1e-05

def split_columns(matrix, pieces):
    rows_n, cols_n = matrix.shape
    return matrix.reshape(rows_n, pieces, cols_n // pieces).transpose(1, 0, 2)

def split_rows(matrix, pieces):
    return matrix.reshape(pieces, matrix.shape[0] // pieces, matrix.shape[1])

def split_rows_flipped(matrix, pieces):
    return split_rows(matrix, pieces).transpose(0, 2, 1)

def blocked_sum(stack_left, stack_right):

    def add_block(running, operands):
        partial_value = jnp.dot(operands[0], operands[1], preferred_element_type=jnp.float32)
        rounded = lax.optimization_barrier(partial_value.astype(jnp.bfloat16))
        return (running + rounded.astype(jnp.float32), None)
    start_value = jnp.zeros((stack_left.shape[1], stack_right.shape[2]), jnp.float32)
    return lax.scan(add_block, start_value, (stack_left, stack_right))[0]

def widen(values):
    return lax.optimization_barrier(values).astype(jnp.float32)

def reference(text_states, latents, w_query, w_key, w_value, w_output, gate_logit, image_index, latent_count, grad_output):
    states = text_states.astype(jnp.float32)
    energy = lax.optimization_barrier(jnp.sum(states * states, axis=1, keepdims=True))
    inv_rms = lax.rsqrt(energy / D + EPS)
    normed = (states * inv_rms).astype(jnp.bfloat16)
    queries = blocked_sum(split_columns(normed, N_AL), split_rows(w_query, N_AL)).astype(jnp.bfloat16)
    key_proj = jnp.dot(latents, w_key, preferred_element_type=jnp.float32).astype(jnp.bfloat16)
    value_proj = jnp.dot(latents, w_value, preferred_element_type=jnp.float32).astype(jnp.bfloat16)
    latent_slot = jnp.arange(NL, dtype=jnp.int32)
    latent_image = latent_slot // LAT
    count_each = jnp.repeat(latent_count, LAT, total_repeat_length=NL)
    allowed_pair = (image_index[:, None] == latent_image[None, :]) & ((latent_slot % LAT)[None, :] < count_each[None, :])
    score_scale = 1.0 / math.sqrt(HS)
    query_heads = widen(queries).reshape(TOKENS, HEADS, HS)
    key_heads = widen(key_proj).reshape(NL, HEADS, HS)
    value_heads = widen(value_proj).reshape(NL, HEADS, HS)
    scores = jnp.einsum('thd,nhd->thn', query_heads, key_heads) * score_scale
    raised = jnp.where(allowed_pair[:, None, :], jnp.exp(scores), 0.0)
    attend_prob = raised / lax.optimization_barrier(jnp.sum(raised, axis=2, keepdims=True))
    attend_low = widen(attend_prob.astype(jnp.bfloat16))
    attended = jnp.einsum('thn,nhd->thd', attend_low, value_heads).reshape(TOKENS, HD).astype(jnp.bfloat16)
    branch_out = blocked_sum(split_columns(attended, N_IA), split_rows(w_output, N_IA))
    gate_value = jnp.tanh(gate_logit.astype(jnp.float32))
    mixed = (states + gate_value * branch_out).astype(jnp.bfloat16)
    upstream = grad_output.astype(jnp.float32)
    grad_gate = lax.optimization_barrier(jnp.sum(upstream * branch_out * (1.0 - gate_value * gate_value), axis=0))
    branch_grad = (upstream * gate_value).astype(jnp.bfloat16)
    grad_w_output = blocked_sum(split_rows_flipped(attended, N_JA), split_rows(branch_grad, N_JA))
    attended_grad = blocked_sum(split_columns(branch_grad, N_AL), split_rows(w_output.T, N_AL)).astype(jnp.bfloat16)
    grad_heads = widen(attended_grad).reshape(TOKENS, HEADS, HS)
    prob_grad = jnp.einsum('thd,nhd->thn', grad_heads, value_heads)
    score_grad = attend_prob * (prob_grad - lax.optimization_barrier(jnp.sum(attend_prob * prob_grad, axis=2, keepdims=True)))
    score_low = widen(score_grad.astype(jnp.bfloat16))
    query_grad = (jnp.einsum('thn,nhd->thd', score_low, key_heads) * score_scale).reshape(TOKENS, HD).astype(jnp.bfloat16)
    key_grad = (jnp.einsum('thn,thd->nhd', score_low, query_heads) * score_scale).reshape(NL, HD).astype(jnp.bfloat16)
    value_grad = jnp.einsum('thn,thd->nhd', attend_low, grad_heads).reshape(NL, HD).astype(jnp.bfloat16)
    grad_w_query = blocked_sum(split_rows_flipped(normed, N_JA), split_rows(query_grad, N_JA))
    normed_grad = blocked_sum(split_columns(query_grad, N_IA), split_rows(w_query.T, N_IA))
    inner_sum = lax.optimization_barrier(jnp.sum(normed_grad * states, axis=1, keepdims=True))
    cubed = inv_rms * inv_rms * inv_rms
    grad_states = (upstream + inv_rms * normed_grad - states * cubed * inner_sum / D).astype(jnp.bfloat16)
    stack_left = jnp.concatenate((split_columns(key_grad, N_IA), split_columns(value_grad, N_IA)), axis=2)
    stack_right = jnp.concatenate((split_rows(w_key.T, N_IA), split_rows(w_value.T, N_IA)), axis=1)
    grad_latents = blocked_sum(stack_left, stack_right).astype(jnp.bfloat16)
    grad_w_key = jnp.dot(latents.T, key_grad, preferred_element_type=jnp.float32)
    grad_w_value = jnp.dot(latents.T, value_grad, preferred_element_type=jnp.float32)
    return (mixed, grad_states, grad_latents, grad_w_query, grad_w_key, grad_w_value, grad_w_output, grad_gate)
```

```python
import functools
import math

import jax
import jax.numpy as jnp
from jax import lax
from jax.experimental import pallas as pl
from jax.experimental.pallas import tpu as pltpu
from jax.sharding import PartitionSpec as P

MESH = pl.DeviceIdType.MESH
D = 8192
EPS = 1e-05
BF = jnp.bfloat16
F32 = jnp.float32
IMGS = 4
HS = 128
CH = 2


def dot(a, b, ca, cb):
    return lax.dot_general(a, b, (((ca,), (cb,)), ((), ())), preferred_element_type=F32)


def loop(lo, hi, f):
    lax.fori_loop(lo, hi, lambda i, c: (f(i), c)[1], 0)


def kernel(sizes, feats, *refs):
    NI, NJ, NZ, NX = sizes
    (
        st_ref, lat_ref, wq_ref, wk_ref, wv_ref, wo_ref, gate_ref, img_ref, cnt_ref, up_ref,
        mixed_ref, gst_ref, glat_ref, gwq_ref, gwk_ref, gwv_ref, gwo_ref, gg_ref,
    ) = refs[:18]
    sc = list(refs[18:])
    (
        W, strow, brrow, latg, latc, latb, latt,
        kv_p, kv_rx, kv_zs, kv_rz, kv_js, kv_rj, kv_full,
        lg_p, lg_rx, lg_zs, lg_rz, lg_js, lg_rj, lg_full,
        q_p, q_rx, q_zs, q_rz, qs,
        a_p, a_rx, a_zs, a_rz, gs,
        e_p, e_rx, e_zs, e_rz,
        atrow, qgrow, innr, rin,
        outp, outr, normp, normr,
        gg_p, gg_r, ggj, ggj_r,
        gp, grr, grl,
        gl, glr, gls, glf,
        prob, probl,
        ssem, rsem,
    ) = sc
    NA = NZ * NX
    TB, DL = st_ref.shape
    WD = wq_ref.shape[1]
    WB = wq_ref.shape[0]
    HL = WD // HS
    LR = lat_ref.shape[0]
    LI = NI * LR
    NL = NJ * LI
    LB = NL // NA
    LAT = NL // IMGS
    CB = 2 * HL
    TR = NI * TB
    scale = 1.0 / math.sqrt(HS)

    ia, ja, al = lax.axis_index("ia"), lax.axis_index("ja"), lax.axis_index("al")
    x, zh = al % NX, al // NX
    me = {"ia": ia, "ja": ja, "al": al}
    size = {"ia": NI, "ja": NJ}
    zdev = {"al": (1 - zh) * NX + x}
    zal = (1 - zh) * NX + x

    used = [0]

    def take(n):
        used[0] += n
        assert used[0] <= ssem.shape[0]
        return used[0] - n

    drains = []

    def copy(src, dst, i, dev):
        return pltpu.make_async_remote_copy(
            src_ref=src, dst_ref=dst, send_sem=ssem.at[i], recv_sem=rsem.at[i],
            device_id=dev, device_id_type=MESH,
        )

    class Exchange:
        def __init__(self, axis, src, dst):
            self.axis, self.src, self.dst = axis, src, dst
            self.n = NX if axis == "x" else size[axis]
            self.base = take(self.n)
            self.me = x if axis == "x" else me[axis]

        def one(self, k, sending):
            peer = (self.me + k) % self.n if sending else (self.me - k + self.n) % self.n
            dev = {"al": zh * NX + peer} if self.axis == "x" else {self.axis: peer}
            if sending:
                return copy(self.src(peer), self.dst(self.me, k), self.base + k, dev)
            return copy(self.src(peer), self.dst(peer, k), self.base + k, dev)

        def start(self):
            loop(1, self.n, lambda k: self.one(k, True).start())
            drains.append(lambda: loop(1, self.n, lambda k: self.one(k, True).wait_send()))

        def wait(self):
            loop(1, self.n, lambda k: self.one(k, False).wait_recv())

    class Swap:
        def __init__(self, src, dst, landed):
            self.i = take(1)
            self.c = copy(src, dst, self.i, zdev)
            self.r = copy(src, landed, self.i, zdev)

        def start(self):
            if NZ == 2:
                self.c.start()
                drains.append(lambda: self.c.wait_send())

        def wait(self):
            if NZ == 2:
                self.r.wait_recv()

    class Scatter:
        def __init__(self, p, rx, zs, rz):
            self.p, self.rx, self.zs, self.rz = p, rx, zs, rz
            self.ex = Exchange("x", lambda peer: p.at[peer], lambda s, k: rx.at[k])
            self.sw = Swap(zs.at[1 - zh] if NZ == 2 else zs.at[0], rz, rz)

        def s1(self):
            self.ex.start()

        def s2(self):
            self.ex.wait()
            t = self.p[x].astype(F32)
            for k in range(1, NX):
                t = t + self.rx[k].astype(F32)
            self.zs[...] = t.astype(self.zs.dtype)
            self.sw.start()

        def s3(self):
            self.sw.wait()
            t = self.zs[zh].astype(F32)
            if NZ == 2:
                t = t + self.rz[...].astype(F32)
            return t

    class Gather:
        def __init__(self, buf):
            self.sw = Swap(buf.at[al], buf.at[al], buf.at[zal])
            self.e1 = Exchange("x", lambda peer: buf.at[al], lambda s, k: buf.at[zh * NX + s])
            self.e2 = Exchange("x", lambda peer: buf.at[zal], lambda s, k: buf.at[(1 - zh) * NX + s])

        def s1(self):
            self.sw.start()
            self.e1.start()

        def s2(self):
            if NZ == 2:
                self.sw.wait()
                self.e2.start()

        def s3(self):
            self.e1.wait()
            if NZ == 2:
                self.e2.wait()

    class AllSum:
        def __init__(self, p, rx, zs, rz, js, rj, full):
            self.sct = Scatter(p, rx, zs, rz)
            self.js, self.rj, self.full = js, rj, full
            self.ex = Exchange("ja", lambda peer: js.at[peer], lambda s, k: rj.at[k])
            self.ag = Exchange("ja", lambda peer: full.at[al, ja], lambda s, k: full.at[al, s])
            self.gat = Gather(full)

        def s1(self):
            self.sct.s1()

        def s2(self):
            self.sct.s2()

        def s3(self):
            self.js[...] = self.sct.s3().astype(BF)
            self.ex.start()

        def s4(self):
            self.ex.wait()
            t = self.js[ja].astype(F32)
            for k in range(1, NJ):
                t = t + self.rj[k].astype(F32)
            self.full[al, ja] = t.astype(BF)
            self.ag.start()

        def s5(self):
            self.ag.wait()
            self.gat.s1()

        def s6(self):
            self.gat.s2()

        def s7(self):
            self.gat.s3()

    T = NJ * CH
    WR, WL = take(2 * T), take(2 * T)
    nr, nl = (ja + 1) * CH, (NJ - ja) * CH

    def item_right(t):
        m, r = t // nr, t % nr
        return m, r, ja - r // CH, r % CH

    def item_left(t):
        m, r = t // nl, t % nl
        return m, r, ja + r // CH, r % CH

    def line_copy(base, m, s, c, to):
        piece = W.at[m, s, c]
        return copy(piece, piece, base + (m * NJ + s) * CH + c, {"ja": to})

    def line_step(t):
        @pl.when(t < 2 * nr)
        def _():
            m, r, s, c = item_right(t)

            @pl.when(r >= CH)
            def _():
                line_copy(WR, m, s, c, ja - 1).wait_recv()

            @pl.when(ja < NJ - 1)
            def _():
                line_copy(WR, m, s, c, ja + 1).start()

        @pl.when(t < 2 * nl)
        def _():
            m, r, s, c = item_left(t)

            @pl.when(r >= CH)
            def _():
                line_copy(WL, m, s, c, ja + 1).wait_recv()

            @pl.when(ja > 0)
            def _():
                line_copy(WL, m, s, c, ja - 1).start()

    def line_drain(t):
        @pl.when((t < 2 * nr) & (ja < NJ - 1))
        def _():
            m, r, s, c = item_right(t)
            line_copy(WR, m, s, c, ja + 1).wait_send()

        @pl.when((t < 2 * nl) & (ja > 0))
        def _():
            m, r, s, c = item_left(t)
            line_copy(WL, m, s, c, ja - 1).wait_send()

    drains.append(lambda: loop(0, 2 * T, line_drain))

    def line(lo, hi):
        loop(lo * CH, hi * CH, line_step)

    SR, SL = take(2 * NJ), take(2 * NJ)

    def sum_copy(base, buf, m, d, to, src=None):
        return copy(buf.at[m, d] if src is None else src, buf.at[m, d], base + m * NJ + d, {"ja": to})

    def sum_step(m, t):
        @pl.when((t >= ja) & (t < NJ - 1))
        def _():
            d = NJ - 1 - t + ja

            @pl.when(ja == 0)
            def _():
                sum_copy(SR, grr, m, d, ja + 1, gp.at[m, d]).start()

            @pl.when(ja > 0)
            def _():
                sum_copy(SR, grr, m, d, ja - 1).wait_recv()
                grr[m, d] = (grr[m, d].astype(F32) + gp[m, d].astype(F32)).astype(BF)
                sum_copy(SR, grr, m, d, ja + 1).start()

        @pl.when((t >= NJ - 1 - ja) & (t < NJ - 1))
        def _():
            d = t - (NJ - 1 - ja)

            @pl.when(ja == NJ - 1)
            def _():
                sum_copy(SL, grl, m, d, ja - 1, gp.at[m, d]).start()

            @pl.when(ja < NJ - 1)
            def _():
                sum_copy(SL, grl, m, d, ja + 1).wait_recv()
                grl[m, d] = (grl[m, d].astype(F32) + gp[m, d].astype(F32)).astype(BF)
                sum_copy(SL, grl, m, d, ja - 1).start()

    def sum_drain(m, t):
        @pl.when((t >= ja) & (t < NJ - 1))
        def _():
            d = NJ - 1 - t + ja
            sum_copy(SR, grr, m, d, ja + 1).wait_send()

        @pl.when((t >= NJ - 1 - ja) & (t < NJ - 1))
        def _():
            d = t - (NJ - 1 - ja)
            sum_copy(SL, grl, m, d, ja - 1).wait_send()

    def sum_line(m, lo, hi):
        loop(lo, hi, lambda t: sum_step(m, t))

    def sum_end(m):
        t = gp[m, ja].astype(F32)

        @pl.when(ja > 0)
        def _():
            sum_copy(SR, grr, m, ja, ja - 1).wait_recv()

        @pl.when(ja < NJ - 1)
        def _():
            sum_copy(SL, grl, m, ja, ja + 1).wait_recv()

        t = t + jnp.where(ja > 0, grr[m, ja].astype(F32), 0.0)
        t = t + jnp.where(ja < NJ - 1, grl[m, ja].astype(F32), 0.0)
        drains.append(lambda: loop(0, NJ, lambda t: sum_drain(m, t)))
        return t

    ex_lat = Exchange("ia", lambda peer: latg.at[ia], lambda s, k: latg.at[s])
    ex_l2 = Exchange("ja", lambda peer: latc.at[peer], lambda s, k: latb.at[s])
    ex_st = Exchange("ia", lambda peer: strow.at[ia], lambda s, k: strow.at[s])
    ex_br = Exchange("ia", lambda peer: brrow.at[ia], lambda s, k: brrow.at[s])
    kv = AllSum(kv_p, kv_rx, kv_zs, kv_rz, kv_js, kv_rj, kv_full)
    lg = AllSum(lg_p, lg_rx, lg_zs, lg_rz, lg_js, lg_rj, lg_full)
    q_s = Scatter(q_p, q_rx, q_zs, q_rz)
    a_s = Scatter(a_p, a_rx, a_zs, a_rz)
    e_ex = Exchange("x", lambda peer: e_p, lambda s, k: e_rx.at[k])
    e_sw = Swap(e_zs, e_rz, e_rz)
    at_g, qg_g, in_g = Gather(atrow), Gather(qgrow), Gather(innr)
    ex_out = Exchange("ia", lambda peer: outp.at[peer], lambda s, k: outr.at[k])
    ex_norm = Exchange("ia", lambda peer: normp.at[peer], lambda s, k: normr.at[k])
    ex_in = Exchange("ia", lambda peer: innr.at[peer], lambda s, k: rin.at[k])
    ex_gi = Exchange("ia", lambda peer: gg_p, lambda s, k: gg_r.at[k])
    ex_gj = Exchange("ja", lambda peer: ggj, lambda s, k: ggj_r.at[k])
    ex_gl = Exchange("ia", lambda peer: gl.at[peer], lambda s, k: glr.at[k])
    ex_g2 = Exchange("ja", lambda peer: gls.at[peer], lambda s, k: glf.at[s])

    barrier = pltpu.get_barrier_semaphore()
    loop(1, NI, lambda k: pl.semaphore_signal(barrier, 1, device_id={"ia": (ia + k) % NI}, device_id_type=MESH))
    loop(1, NJ, lambda k: pl.semaphore_signal(barrier, 1, device_id={"ja": (ja + k) % NJ}, device_id_type=MESH))
    loop(1, NX, lambda k: pl.semaphore_signal(barrier, 1, device_id={"al": zh * NX + (x + k) % NX}, device_id_type=MESH))
    if NZ == 2:
        pl.semaphore_signal(barrier, 1, device_id=zdev, device_id_type=MESH)
    W[0, ja] = wq_ref[...].reshape(CH, WB // CH, WD)
    strow[ia] = st_ref[...]
    latg[ia] = jnp.zeros((16, DL), BF)
    latg[ia, 0:LR, :] = lat_ref[...]
    gate = jnp.tanh(gate_ref[...])
    brrow[ia] = (up_ref[...].astype(F32) * gate).astype(BF)
    pl.semaphore_wait(barrier, NI - 1 + NJ - 1 + NX - 1 + NZ - 1)

    ex_lat.start()
    line(0, 1)
    ex_st.start()
    W[1, ja] = wo_ref[...].T.reshape(CH, WB // CH, WD)
    ex_br.start()
    line(1, 2)

    ex_lat.wait()
    pick_r = lax.broadcasted_iota(jnp.int32, (LI, NI * 16), 0)
    pick_c = lax.broadcasted_iota(jnp.int32, (LI, NI * 16), 1)
    pick = (pick_c == (pick_r // LR) * 16 + pick_r % LR).astype(F32).astype(BF)
    packed = dot(pick, latg[...].reshape(NI * 16, DL), 1, 0).astype(BF)
    for s in range(NJ):
        latc[s] = packed[:, s * 128 : (s + 1) * 128]
    latb[ja] = latc[ja]
    ex_l2.start()
    line(2, 3)

    ex_l2.wait()
    lat = latb[...].reshape(NL, 128)
    latt[...] = lat.T
    for h in range(CB):
        wref = wk_ref if h < HL else wv_ref
        c = h % HL
        part = dot(lat, wref[:, c * HS : (c + 1) * HS], 1, 0).astype(BF)
        for a in range(NA):
            kv_p[a % NX, a // NX, h] = part[a * LB : (a + 1) * LB]
    kv.s1()
    line(3, 4)

    ex_st.wait()
    states_rows = strow[...].reshape(TR, DL)
    sq = states_rows.astype(F32)
    sq = (sq * sq).astype(BF)
    e_p[...] = dot(jnp.ones((8, DL), BF), sq, 1, 1)[0:1]
    e_ex.start()
    kv.s2()
    line(4, 5)
    kv.s3()
    e_ex.wait()
    t = e_p[...]
    for k in range(1, NX):
        t = t + e_rx[k]
    e_zs[...] = t
    e_sw.start()
    line(5, 6)
    kv.s4()
    line(6, 7)
    kv.s5()
    line(7, 8)
    kv.s6()

    def rows_times(rows, m, p):
        acc = dot(rows, W[m].reshape(DL, WD), 1, 0).astype(BF)
        for a in range(NA):
            p[a % NX, a // NX] = acc[a * TB : (a + 1) * TB]

    rows_times(states_rows, 0, q_p)
    q_s.s1()
    line(8, 9)
    q_s.s2()
    e_sw.wait()
    energy = e_zs[...]
    if NZ == 2:
        energy = energy + e_rz[...]
    inv_row = lax.rsqrt(energy / D + EPS)

    lane = lax.broadcasted_iota(jnp.int32, (TB, TR), 1)
    sub = lax.broadcasted_iota(jnp.int32, (TB, TR), 0)

    def column(block):
        return jnp.sum(jnp.where(lane == block * TB + sub, inv_row, 0.0), axis=1, keepdims=True)

    inv_attn, inv_own = column(al), column(ia)
    line(9, 10)
    kv.s7()
    q = q_s.s3() * inv_attn
    qs[...] = q.astype(BF)

    slot = lax.broadcasted_iota(jnp.int32, (TB, NL), 1)
    image = slot // LAT
    count = jnp.where(image == 0, cnt_ref[0], jnp.where(image == 1, cnt_ref[1], jnp.where(image == 2, cnt_ref[2], cnt_ref[3])))
    allowed = (img_ref[...] == image) & (slot % LAT < count)
    for h in range(HL):
        cols = slice(h * HS, (h + 1) * HS)
        kh = kv_full[:, h].reshape(NL, HS)
        vh = kv_full[:, HL + h].reshape(NL, HS)
        sco = dot(qs[:, cols], kh, 1, 1) * scale
        raised = jnp.where(allowed, jnp.exp(sco), 0.0)
        pr = raised / jnp.sum(raised, axis=1, keepdims=True)
        prob[h] = pr
        probl[h] = pr.astype(BF)
        atrow[al, :, cols] = dot(probl[h], vh, 1, 0).astype(BF)
    at_g.s1()
    line(10, 11)
    at_g.s2()
    ex_br.wait()
    branch_rows = brrow[...].reshape(TR, DL)
    line(11, 16 if NJ == 8 else 2 * NJ)

    def times_rows_t(rows, m, dst):
        for s in range(NJ):
            r = dot(rows, W[m, s].reshape(WB, WD), 1, 1).astype(BF)
            dst[:, :, s * WB : (s + 1) * WB] = r.reshape(NI, TB, WB)

    def grad_parts(left, right, m):
        for s in range(NJ):
            gp[m, s] = dot(left[:, s * WB : (s + 1) * WB], right, 0, 0).astype(BF)

    rows_times(branch_rows, 1, a_p)
    a_s.s1()
    at_g.s3()
    attn_rows = atrow[...].reshape(TR, WD)
    grad_parts(branch_rows, attn_rows, 1)
    sum_line(1, 0, 1)
    a_s.s2()
    times_rows_t(attn_rows, 1, outp)
    ex_out.start()
    sum_line(1, 1, 2)

    grads = a_s.s3()
    gs[...] = grads.astype(BF)
    inner = jnp.zeros((TB, 1), F32)
    for h in range(HL):
        cols = slice(h * HS, (h + 1) * HS)
        kh = kv_full[:, h].reshape(NL, HS)
        vh = kv_full[:, HL + h].reshape(NL, HS)
        gh = gs[:, cols]
        qh = qs[:, cols]
        pg = dot(gh, vh, 1, 1)
        pr = prob[h]
        sg = pr * (pg - jnp.sum(pr * pg, axis=1, keepdims=True))
        sl = sg.astype(BF)
        qg = dot(sl, kh, 1, 0) * scale * inv_attn
        inner = inner + jnp.sum(qg * qh.astype(F32), axis=1, keepdims=True)
        qgrow[al, :, cols] = qg.astype(BF)
        kt = (dot(sl, qh, 0, 0) * scale).astype(BF)
        vt = dot(probl[h], gh, 0, 0).astype(BF)
        for a in range(NA):
            lg_p[a % NX, a // NX, h] = kt[a * LB : (a + 1) * LB]
            lg_p[a % NX, a // NX, HL + h] = vt[a * LB : (a + 1) * LB]
    lane1 = lax.broadcasted_iota(jnp.int32, (TB, 128), 1)
    sub1 = lax.broadcasted_iota(jnp.int32, (TB, 128), 0)
    innr[al] = jnp.sum(jnp.where(lane1 == sub1, inner, 0.0), axis=0, keepdims=True)
    qg_g.s1()
    in_g.s1()
    lg.s1()
    sum_line(1, 2, 3)
    qg_g.s2()
    in_g.s2()
    lg.s2()
    sum_line(1, 3, 4)

    ex_out.wait()
    branch = outp[ia].astype(F32)
    for k in range(1, NI):
        branch = branch + outr[k].astype(F32)
    up = up_ref[...].astype(F32)
    mixed_ref[...] = (st_ref[...].astype(F32) + gate * branch).astype(BF)
    gg_p[...] = jnp.sum(up * branch * (1.0 - gate * gate), axis=0, keepdims=True)
    ex_gi.start()

    qg_g.s3()
    in_g.s3()
    qg_rows = qgrow[...].reshape(TR, WD)
    grad_parts(states_rows, qg_rows, 0)
    sum_line(1, 4, 5)
    sum_line(0, 0, 1)
    times_rows_t(qg_rows, 0, normp)
    ex_norm.start()
    ex_in.start()
    lg.s3()
    sum_line(1, 5, 6)
    sum_line(0, 1, 2)
    ex_gi.wait()
    t = gg_p[...]
    for k in range(1, NI):
        t = t + gg_r[k]
    ggj[...] = t
    ex_gj.start()
    lg.s4()
    sum_line(1, 6, NJ)
    sum_line(0, 2, 3)
    lg.s5()
    gwo_ref[...] = sum_end(1).T.astype(F32)
    sum_line(0, 3, 4)
    lg.s6()
    ex_norm.wait()
    ex_in.wait()
    ng = normp[ia].astype(F32)
    inner = innr[ia]
    for k in range(1, NI):
        ng = ng + normr[k].astype(F32)
        inner = inner + rin[k]
    inner = jnp.sum(jnp.where(lane1 == sub1, inner, 0.0), axis=1, keepdims=True)
    gst_ref[...] = (up + ng - st_ref[...].astype(F32) * (inv_own * inner / D)).astype(BF)
    sum_line(0, 4, 5)
    lg.s7()
    total = jnp.zeros((NL, 128), F32)
    for h in range(HL):
        cols = slice(h * HS, (h + 1) * HS)
        kg = lg_full[:, h].reshape(NL, HS)
        vg = lg_full[:, HL + h].reshape(NL, HS)
        total = total + dot(kg, wk_ref[:, cols], 1, 1) + dot(vg, wv_ref[:, cols], 1, 1)
    rowi = lax.broadcasted_iota(jnp.int32, (NL, NL), 0)
    coli = lax.broadcasted_iota(jnp.int32, (NL, NL), 1)
    from_row = ((rowi // LR) % NJ) * LI + (rowi // (LR * NJ)) * LR + rowi % LR
    perm = (coli == from_row).astype(F32).astype(BF)
    gl[...] = dot(perm, total.astype(BF), 1, 0).astype(BF).reshape(NI, NJ * LR, 128)
    ex_gl.start()
    sum_line(0, 5, 6)
    for h in range(HL):
        cols = slice(h * HS, (h + 1) * HS)
        gwk_ref[:, cols] = dot(latt[...], lg_full[:, h].reshape(NL, HS), 1, 0)
        gwv_ref[:, cols] = dot(latt[...], lg_full[:, HL + h].reshape(NL, HS), 1, 0)
    ex_gl.wait()
    t = gl[ia].astype(F32)
    for k in range(1, NI):
        t = t + glr[k].astype(F32)
    wide_r = lax.broadcasted_iota(jnp.int32, (NJ * 16, NJ * LR), 0)
    wide_c = lax.broadcasted_iota(jnp.int32, (NJ * 16, NJ * LR), 1)
    wide = ((wide_r // 16 * LR + wide_r % 16 == wide_c) & (wide_r % 16 < LR)).astype(F32).astype(BF)
    gls[...] = dot(wide, t.astype(BF), 1, 0).astype(BF).reshape(NJ, 16, 128)
    glf[ja] = gls[ja]
    ex_g2.start()
    sum_line(0, 6, NJ)
    ex_gj.wait()
    t = ggj[...]
    for k in range(1, NJ):
        t = t + ggj_r[k]
    gg_ref[...] = t
    ex_g2.wait()
    for s in range(NJ):
        glat_ref[:, s * 128 : (s + 1) * 128] = glf[s, 0:LR, :]
    gwq_ref[...] = sum_end(0).astype(F32)
    for f in drains:
        f()


def run(sizes, *args):
    NI, NJ, NZ, NX = sizes
    st, lat, wq, wk, wv, wo, gate, img, cnt, up = args
    NA = NZ * NX
    TB, DL = st.shape
    WB, WD = wq.shape
    HL = WD // HS
    LR = lat.shape[0]
    LI = NI * LR
    NL = NJ * LI
    LB = NL // NA
    CB = 2 * HL
    TR = NI * TB
    assert CB == NJ and NI == NA and NZ <= 2 and DL == NJ * 128 and WB == 128
    vm = lambda dt, *s: pltpu.VMEM(s, dt)

    def allsum():
        return [
            vm(BF, NX, NZ, CB, LB, 128), vm(BF, NX, NZ, CB, LB, 128), vm(BF, NZ, CB, LB, 128), vm(BF, CB, LB, 128),
            vm(BF, CB, LB, 128), vm(BF, NJ, LB, 128), vm(BF, NA, CB, LB, 128),
        ]

    def scatter():
        return [
            vm(BF, NX, NZ, TB, WD), vm(BF, NX, NZ, TB, WD), vm(BF, NZ, TB, WD), vm(BF, TB, WD), vm(BF, TB, WD),
        ]

    scratch = [
        vm(BF, 2, NJ, CH, WB // CH, WD), vm(BF, NI, TB, DL), vm(BF, NI, TB, DL),
        vm(BF, NI, 16, DL), vm(BF, NJ, LI, 128), vm(BF, NJ, LI, 128), vm(BF, 128, NL),
        *allsum(), *allsum(), *scatter(), *scatter(),
        vm(F32, 1, TR), vm(F32, NX, 1, TR), vm(F32, 1, TR), vm(F32, 1, TR),
        vm(BF, NA, TB, WD), vm(BF, NA, TB, WD), vm(F32, NA, 1, 128), vm(F32, NI, 1, 128),
        vm(BF, NI, TB, DL), vm(BF, NI, TB, DL), vm(BF, NI, TB, DL), vm(BF, NI, TB, DL),
        vm(F32, 1, DL), vm(F32, NI, 1, DL), vm(F32, 1, DL), vm(F32, NJ, 1, DL),
        vm(BF, 2, NJ, WB, WD), vm(BF, 2, NJ, WB, WD), vm(BF, 2, NJ, WB, WD),
        vm(BF, NI, NJ * LR, 128), vm(BF, NI, NJ * LR, 128), vm(BF, NJ, 16, 128), vm(BF, NJ, 16, 128),
        vm(F32, HL, TB, NL), vm(BF, HL, TB, NL),
        pltpu.SemaphoreType.DMA((320,)), pltpu.SemaphoreType.DMA((320,)),
    ]
    v, s = pl.BlockSpec(memory_space=pltpu.VMEM), pl.BlockSpec(memory_space=pltpu.SMEM)
    shape = jax.ShapeDtypeStruct
    out = pl.pallas_call(
        functools.partial(kernel, sizes, DL),
        out_shape=(
            shape((TB, DL), BF), shape((TB, DL), BF), shape((LR, DL), BF), shape((WB, WD), F32),
            shape((WB, WD), F32), shape((WB, WD), F32), shape((WD, WB), F32), shape((1, DL), F32),
        ),
        in_specs=[v] * 8 + [s, v],
        out_specs=tuple([v] * 8),
        scratch_shapes=scratch,
        compiler_params=pltpu.CompilerParams(collective_id=0, has_side_effects=True, vmem_limit_bytes=56 * 2**20),
    )(st, lat, wq, wk, wv, wo, gate.reshape(1, DL), img.reshape(TB, 1), cnt, up)
    return (*out[:7], out[7].reshape(DL))


def solution(mesh, sizes=None):
    if sizes is None:
        sizes = (mesh.shape["ia"], mesh.shape["ja"], 2, mesh.shape["al"] // 2)
    tokens = P(("ja", "ia"), "al")
    weight = P(("al", "ja"), "ia")
    second = P("ia", ("al", "ja"))
    return jax.shard_map(
        functools.partial(run, sizes),
        mesh=mesh,
        in_specs=(tokens, tokens, weight, weight, weight, second, P("al"), P(("ja", "al")), P(), tokens),
        out_specs=(tokens, tokens, tokens, weight, weight, weight, second, P("al")),
        check_vma=False,
    )
```

```python
import functools
import math

import jax
import jax.numpy as jnp
from jax import lax
from jax.experimental import pallas as pl
from jax.experimental.pallas import tpu as pltpu
from jax.sharding import PartitionSpec as P

MESH = pl.DeviceIdType.MESH
D = 8192
EPS = 1e-05
BF = jnp.bfloat16
F32 = jnp.float32
IMGS = 4
HS = 128


def dot(a, b, ca, cb):
    return lax.dot_general(a, b, (((ca,), (cb,)), ((), ())), preferred_element_type=F32)


def loop(lo, hi, f):
    lax.fori_loop(lo, hi, lambda i, c: (f(i), c)[1], 0)


def kernel(sizes, *refs):
    NI, NJ, NZ, NX = sizes
    (
        st_ref, lat_ref, wq_ref, wk_ref, wv_ref, wo_ref, gate_ref, img_ref, cnt_ref, up_ref,
        mixed_ref, gst_ref, glat_ref, gwq_ref, gwk_ref, gwv_ref, gwo_ref, gg_ref,
    ) = refs[:18]
    (
        W, latg, latc, latb, latt,
        s0, s1, s2, s3, strow,
        b0, b1, b2, b3, brrow,
        kv_p, kv_rx, kv_zs, kv_rz, kv_full,
        lg_p, lg_rx, lg_zs, lg_rz, lg_full,
        q_p, q_rr, q_rl, qs,
        a_p, a_rr, a_rl, gs,
        e_p, e_r, im_z, im_x,
        atrow, qgrow, innr, rin,
        outp, outr, out1, out2, out3,
        normp, normr, norm1, norm2, norm3,
        gg_p, gg_r, ggj, ggj_r,
        gp, gpr,
        gl, glr, gls, glf,
        prob, probl,
        ssem, rsem,
    ) = refs[18:]
    NA, NR = NZ * NX, NZ * NJ
    TB, DL = st_ref.shape
    WB, WD = wq_ref.shape
    HL = WD // HS
    LR = lat_ref.shape[0]
    LI = NI * LR
    NL = NJ * LI
    LB = NL // NA
    LAT = NL // IMGS
    CB = 2 * HL
    TG = NR * TB
    DG = NX * WB
    scale = 1.0 / math.sqrt(HS)

    ia, ja, al = lax.axis_index("ia"), lax.axis_index("ja"), lax.axis_index("al")
    x, zh = al % NX, al // NX
    z = zh * NJ + ja
    place = {"ia": (ia, NI), "ja": (ja, NJ), "x": (x, NX), "z": (z, NR)}

    def device(axis, i):
        if axis == "x":
            return {"al": zh * NX + i}
        if axis == "z":
            return {"ja": i % NJ, "al": (i // NJ) * NX + x}
        return {axis: i}

    used = [0]
    drains = []

    def take(n):
        used[0] += n
        assert used[0] <= ssem.shape[0]
        return used[0] - n

    def copy(src, dst, i, dev):
        return pltpu.make_async_remote_copy(
            src_ref=src, dst_ref=dst, send_sem=ssem.at[i], recv_sem=rsem.at[i],
            device_id=dev, device_id_type=MESH,
        )

    class Exchange:
        def __init__(self, axis, src, dst):
            self.axis, self.src, self.dst = axis, src, dst
            self.me, self.n = place[axis]
            self.base = take(self.n)

        def out(self, k):
            peer = (self.me + k) % self.n
            return copy(self.src(peer), self.dst(self.me, k), self.base + k, device(self.axis, peer))

        def into(self, k):
            peer = (self.me - k + self.n) % self.n
            return copy(self.src(peer), self.dst(peer, k), self.base + k, device(self.axis, peer))

        def start(self):
            loop(1, self.n, lambda k: self.out(k).start())
            drains.append(lambda: loop(1, self.n, lambda k: self.out(k).wait_send()))

        def wait(self):
            loop(1, self.n, lambda k: self.into(k).wait_recv())

    FAR, NEAR = NR // 2, NR - 1 - NR // 2
    right, left = device("z", (z + 1) % NR), device("z", (z + NR - 1) % NR)

    class RingSum:
        def __init__(self, p, rr, rl):
            self.p, self.rr, self.rl = p, rr, rl
            self.r, self.l = take(FAR), take(NEAR)

        def go_right(self, s, src):
            return copy(src, self.rr.at[s], self.r + s, right)

        def go_left(self, s, src):
            return copy(src, self.rl.at[s], self.l + s, left)

        def step(self, s):
            p, rr, rl = self.p, self.rr, self.rl
            if s == 0:
                self.go_right(0, p.at[(z + FAR) % NR]).start()
                self.go_left(0, p.at[(z + NR - NEAR) % NR]).start()
                return
            if s < FAR:
                self.go_right(s - 1, rr.at[s - 1]).wait_recv()
                rr[s - 1] = (rr[s - 1].astype(F32) + p[(z + FAR - s) % NR].astype(F32)).astype(BF)
                self.go_right(s, rr.at[s - 1]).start()
            if s < NEAR:
                self.go_left(s - 1, rl.at[s - 1]).wait_recv()
                rl[s - 1] = (rl[s - 1].astype(F32) + p[(z + NR - NEAR + s) % NR].astype(F32)).astype(BF)
                self.go_left(s, rl.at[s - 1]).start()

        def end(self):
            self.go_right(FAR - 1, self.rr.at[FAR - 1]).wait_recv()
            self.go_left(NEAR - 1, self.rl.at[NEAR - 1]).wait_recv()

            def drain():
                for s in range(FAR):
                    self.go_right(s, self.rr.at[s]).wait_send()
                for s in range(NEAR):
                    self.go_left(s, self.rl.at[s]).wait_send()

            drains.append(drain)
            return self.p[z].astype(F32) + self.rr[FAR - 1].astype(F32) + self.rl[NEAR - 1].astype(F32)

    class RingGather:
        def __init__(self, buf):
            self.buf = buf
            self.r, self.l = take(FAR), take(NEAR)

        def go_right(self, s):
            b = self.buf.at[(z - s + NR) % NR]
            return copy(b, b, self.r + s, right)

        def go_left(self, s):
            b = self.buf.at[(z + s) % NR]
            return copy(b, b, self.l + s, left)

        def step(self, s):
            if s < FAR:
                if s > 0:
                    self.go_right(s - 1).wait_recv()
                self.go_right(s).start()
            if s < NEAR:
                if s > 0:
                    self.go_left(s - 1).wait_recv()
                self.go_left(s).start()

        def end(self):
            self.go_right(FAR - 1).wait_recv()
            self.go_left(NEAR - 1).wait_recv()

            def drain():
                for s in range(FAR):
                    self.go_right(s).wait_send()
                for s in range(NEAR):
                    self.go_left(s).wait_send()

            drains.append(drain)

    class AllSum:
        def __init__(self, p, rx, zs, rz, full):
            self.p, self.rx, self.zs, self.rz, self.full = p, rx, zs, rz, full
            self.x1 = Exchange("x", lambda peer: p.at[peer], lambda s, k: rx.at[k])
            self.z1 = Exchange("z", lambda peer: zs.at[peer // NJ, peer % NJ], lambda s, k: rz.at[k])
            self.z2 = Exchange("z", lambda peer: full.at[x, zh, ja], lambda s, k: full.at[x, s // NJ, s % NJ])
            self.x2 = Exchange("x", lambda peer: full.at[x], lambda s, k: full.at[s])

        def a(self):
            self.x1.start()

        def b(self):
            self.x1.wait()
            t = self.p[x].astype(F32)
            for k in range(1, NX):
                t = t + self.rx[k].astype(F32)
            self.zs[...] = t.astype(BF)
            self.z1.start()

        def c(self):
            self.z1.wait()
            t = self.zs[zh, ja].astype(F32)
            for k in range(1, NR):
                t = t + self.rz[k].astype(F32)
            self.full[x, zh, ja] = t.astype(BF)
            self.z2.start()

        def d(self):
            self.z2.wait()
            self.x2.start()

        def e(self):
            self.x2.wait()

        def head(self, h):
            return jnp.concatenate([self.full[a % NX, a // NX, h] for a in range(NA)], axis=0)

    class Spread:
        def __init__(self, t0, t1, t2, t3, rows):
            self.t0, self.t1, self.t2, self.t3, self.rows = t0, t1, t2, t3, rows
            self.z = Exchange("ja", lambda peer: t0.at[peer], lambda s, k: t1.at[s // NZ, s % NZ])
            self.x = Exchange("x", lambda peer: t1.at[peer], lambda s, k: t2.at[s])
            self.y = Exchange("ia", lambda peer: t3.at[ia], lambda s, k: t3.at[s])

        def load(self, v):
            for s in range(NJ):
                self.t0[s] = v[:, s * WB : (s + 1) * WB]
            self.t1[ja // NZ, ja % NZ] = self.t0[ja]

        def a(self):
            self.z.start()

        def b(self):
            self.z.wait()
            self.x.start()

        def c(self):
            self.x.wait()
            self.t2[x] = self.t1[x]
            self.t3[ia] = self.t2[...]
            self.y.start()

        def d(self):
            self.y.wait()
            for k in range(NX):
                for j in range(NZ):
                    self.rows[j * NI * TB : (j + 1) * NI * TB, k * WB : (k + 1) * WB] = self.t3[:, k, j].reshape(NI * TB, WB)

    class Collect:
        def __init__(self, p, r, t1, t2, t3):
            self.p, self.r, self.t1, self.t2, self.t3 = p, r, t1, t2, t3
            self.y = Exchange("ia", lambda peer: p.at[peer], lambda s, k: r.at[k])
            self.x = Exchange("x", lambda peer: t1.at[peer], lambda s, k: t2.at[s])
            self.z = Exchange("ja", lambda peer: t2.at[peer // NZ, peer % NZ], lambda s, k: t3.at[s])

        def a(self, rows, m):
            for k in range(NX):
                v = dot(rows, W[m, k], 1, 1).astype(BF)
                for j in range(NZ):
                    self.p[:, k, j] = v[j * NI * TB : (j + 1) * NI * TB].reshape(NI, TB, WB)
            self.y.start()

        def b(self, correct=None):
            self.y.wait()
            t = self.p[ia].astype(F32)
            for k in range(1, NI):
                t = t + self.r[k].astype(F32)
            if correct is not None:
                t = correct(t)
            self.t1[...] = t.astype(BF)
            self.t2[x] = self.t1[x]
            self.x.start()

        def c(self):
            self.x.wait()
            self.t3[ja] = self.t2[ja // NZ, ja % NZ]
            self.z.start()

        def d(self):
            self.z.wait()
            return jnp.concatenate([self.t3[s] for s in range(NJ)], axis=1).astype(F32)

    ex_wq = Exchange("x", lambda peer: W.at[0, x], lambda s, k: W.at[0, s])
    ex_wo = Exchange("x", lambda peer: W.at[1, x], lambda s, k: W.at[1, s])
    ex_lat = Exchange("ia", lambda peer: latg.at[ia], lambda s, k: latg.at[s])
    ex_l2 = Exchange("ja", lambda peer: latc.at[peer], lambda s, k: latb.at[s])
    sp_s, sp_b = Spread(s0, s1, s2, s3, strow), Spread(b0, b1, b2, b3, brrow)
    kv = AllSum(kv_p, kv_rx, kv_zs, kv_rz, kv_full)
    lg = AllSum(lg_p, lg_rx, lg_zs, lg_rz, lg_full)
    q_s, a_s = RingSum(q_p, q_rr, q_rl), RingSum(a_p, a_rr, a_rl)
    e_z = Exchange("z", lambda peer: e_p, lambda s, k: e_r.at[k])
    ex_iz = Exchange("z", lambda peer: im_z.at[z], lambda s, k: im_z.at[s])
    ex_ix = Exchange("x", lambda peer: im_x.at[x], lambda s, k: im_x.at[s])
    at_g, qg_g = RingGather(atrow), RingGather(qgrow)
    in_g = Exchange("z", lambda peer: innr.at[ja, zh], lambda s, k: innr.at[s % NJ, s // NJ])
    ex_in = Exchange("ia", lambda peer: innr.at[peer], lambda s, k: rin.at[k])
    c_out, c_norm = Collect(outp, outr, out1, out2, out3), Collect(normp, normr, norm1, norm2, norm3)
    ex_gi = Exchange("ia", lambda peer: gg_p, lambda s, k: gg_r.at[k])
    ex_gj = Exchange("ja", lambda peer: ggj, lambda s, k: ggj_r.at[k])
    ex_gq = Exchange("x", lambda peer: gp.at[0, peer], lambda s, k: gpr.at[0, k])
    ex_go = Exchange("x", lambda peer: gp.at[1, peer], lambda s, k: gpr.at[1, k])
    ex_gl = Exchange("ia", lambda peer: gl.at[peer], lambda s, k: glr.at[k])
    ex_g2 = Exchange("ja", lambda peer: gls.at[peer], lambda s, k: glf.at[s])

    barrier = pltpu.get_barrier_semaphore()
    for axis in ("ia", "x", "z"):
        i, n = place[axis]
        loop(1, n, lambda k: pl.semaphore_signal(barrier, 1, device_id=device(axis, (i + k) % n), device_id_type=MESH))

    lane1 = lax.broadcasted_iota(jnp.int32, (TB, 128), 1)
    sub1 = lax.broadcasted_iota(jnp.int32, (TB, 128), 0)

    def to_row(col):
        return jnp.sum(jnp.where(lane1 == sub1, col, 0.0), axis=0, keepdims=True)

    def to_col(row):
        return jnp.sum(jnp.where(lane1 == sub1, row, 0.0), axis=1, keepdims=True)

    sp_s.load(st_ref[...])
    latg[ia] = jnp.zeros((16, DL), BF)
    latg[ia, 0:LR, :] = lat_ref[...]
    W[0, x] = wq_ref[...]
    gate = jnp.tanh(gate_ref[...])
    sp_b.load((up_ref[...].astype(F32) * gate).astype(BF))
    im_z[z] = to_row(img_ref[...].astype(F32))
    pl.semaphore_wait(barrier, NI - 1 + NX - 1 + NR - 1)

    sp_s.a()
    ex_lat.start()
    sp_b.a()
    ex_wq.start()
    ex_iz.start()
    W[1, x] = wo_ref[...].T
    ex_wo.start()

    sp_s.b()
    ex_lat.wait()
    pick_r = lax.broadcasted_iota(jnp.int32, (LI, NI * 16), 0)
    pick_c = lax.broadcasted_iota(jnp.int32, (LI, NI * 16), 1)
    pick = (pick_c == (pick_r // LR) * 16 + pick_r % LR).astype(F32).astype(BF)
    packed = dot(pick, latg[...].reshape(NI * 16, DL), 1, 0).astype(BF)
    for s in range(NJ):
        latc[s] = packed[:, s * 128 : (s + 1) * 128]
    latb[ja] = latc[ja]
    ex_l2.start()
    sp_b.b()
    sp_s.c()
    sp_b.c()

    ex_l2.wait()
    lat = latb[...].reshape(NL, 128)
    latt[...] = lat.T
    for h in range(CB):
        wref = wk_ref if h < HL else wv_ref
        c = h % HL
        part = dot(lat, wref[:, c * HS : (c + 1) * HS], 1, 0).astype(BF)
        for a in range(NA):
            kv_p[a % NX, a // NX, h] = part[a * LB : (a + 1) * LB]
    kv.a()
    ex_iz.wait()
    im_x[x] = im_z[...]
    ex_ix.start()

    def rows_times(rows, m, p):
        acc = dot(rows, W[m].reshape(DG, WD), 1, 0).astype(BF)
        for d in range(NR):
            p[d] = acc[d * TB : (d + 1) * TB]

    sp_s.d()
    ex_wq.wait()
    rows_times(strow[...], 0, q_p)
    q_s.step(0)
    kv.b()
    sq = strow[...].astype(F32)
    sq = (sq * sq).astype(BF)
    e_p[...] = dot(jnp.ones((8, DG), BF), sq, 1, 1)[0:1]
    e_z.start()
    q_s.step(1)
    sp_b.d()
    ex_wo.wait()
    rows_times(brrow[...], 1, a_p)
    q_s.step(2)
    a_s.step(0)
    kv.c()
    q_s.step(3)
    a_s.step(1)
    q_s.step(4)
    a_s.step(2)
    kv.d()
    q_s.step(5)
    a_s.step(3)
    e_z.wait()
    energy = e_p[...]
    for k in range(1, NR):
        energy = energy + e_r[k]
    inv_row = lax.rsqrt(energy / D + EPS)
    lane = lax.broadcasted_iota(jnp.int32, (TB, TG), 1)
    sub = lax.broadcasted_iota(jnp.int32, (TB, TG), 0)

    def column(block):
        return jnp.sum(jnp.where(lane == block * TB + sub, inv_row, 0.0), axis=1, keepdims=True)

    inv_attn = column(z)
    ex_ix.wait()
    image_col = to_col(im_x[ja % NX, (ja // NX) * NJ + NZ * x + zh])
    slot = lax.broadcasted_iota(jnp.int32, (TB, NL), 1)
    image = slot // LAT
    count = jnp.where(image == 0, cnt_ref[0], jnp.where(image == 1, cnt_ref[1], jnp.where(image == 2, cnt_ref[2], cnt_ref[3])))
    allowed = (image_col == image.astype(F32)) & (slot % LAT < count)
    for s in range(6, FAR):
        q_s.step(s)
        a_s.step(s - 2)
    kv.e()
    q = q_s.end() * inv_attn
    qs[...] = q.astype(BF)
    for h in range(HL):
        cols = slice(h * HS, (h + 1) * HS)
        sco = dot(qs[:, cols], kv.head(h), 1, 1) * scale
        raised = jnp.where(allowed, jnp.exp(sco), 0.0)
        pr = raised / jnp.sum(raised, axis=1, keepdims=True)
        prob[h] = pr
        probl[h] = pr.astype(BF)
        atrow[z, :, cols] = dot(probl[h], kv.head(HL + h), 1, 0).astype(BF)
    at_g.step(0)
    for s in range(max(FAR - 2, 4), FAR):
        a_s.step(s)
    at_g.step(1)

    gs[...] = a_s.end().astype(BF)
    at_g.step(2)
    inner = jnp.zeros((TB, 1), F32)
    for h in range(HL):
        cols = slice(h * HS, (h + 1) * HS)
        kh = kv.head(h)
        gh = gs[:, cols]
        qh = qs[:, cols]
        pg = dot(gh, kv.head(HL + h), 1, 1)
        pr = prob[h]
        sg = pr * (pg - jnp.sum(pr * pg, axis=1, keepdims=True))
        sl = sg.astype(BF)
        qg = dot(sl, kh, 1, 0) * scale * inv_attn
        inner = inner + jnp.sum(qg * qh.astype(F32), axis=1, keepdims=True)
        qgrow[z, :, cols] = qg.astype(BF)
        kt = (dot(sl, qh, 0, 0) * scale).astype(BF)
        vt = dot(probl[h], gh, 0, 0).astype(BF)
        for a in range(NA):
            lg_p[a % NX, a // NX, h] = kt[a * LB : (a + 1) * LB]
            lg_p[a % NX, a // NX, HL + h] = vt[a * LB : (a + 1) * LB]
    qg_g.step(0)
    innr[ja, zh] = to_row(inner)
    in_g.start()
    lg.a()
    at_g.step(3)
    qg_g.step(1)
    at_g.step(4)
    qg_g.step(2)
    lg.b()
    for s in range(5, FAR):
        at_g.step(s)
        qg_g.step(s - 2)
    at_g.end()

    def grad_parts(left_rows, right_rows, m):
        for k in range(NX):
            gp[m, k] = dot(left_rows[:, k * WB : (k + 1) * WB], right_rows, 0, 0).astype(BF)

    def grad_sum(m):
        t = gp[m, x].astype(F32)
        for k in range(1, NX):
            t = t + gpr[m, k].astype(F32)
        return t

    attn_rows = atrow[...].reshape(TG, WD)
    c_out.a(attn_rows, 1)
    for s in range(max(FAR - 2, 3), FAR):
        qg_g.step(s)
    lg.c()
    grad_parts(brrow[...], attn_rows, 1)
    ex_go.start()
    in_g.wait()
    ex_in.start()
    qg_g.end()
    qg_rows = qgrow[...].reshape(TG, WD)
    c_norm.a(qg_rows, 0)
    c_out.b()
    grad_parts(strow[...], qg_rows, 0)
    ex_gq.start()
    lg.d()
    c_out.c()

    def correct(t):
        ex_in.wait()
        own = innr[ia]
        for k in range(1, NI):
            own = own + rin[k]
        parts = []
        for j in range(NZ):
            coef = column(j * NI + ia) * to_col(own[j]) / D
            parts.append(t[:, j] - s2[:, j].astype(F32) * coef[None])
        return jnp.stack(parts, axis=1)

    c_norm.b(correct)
    up = up_ref[...].astype(F32)
    branch = c_out.d()
    mixed_ref[...] = (st_ref[...].astype(F32) + gate * branch).astype(BF)
    gg_p[...] = jnp.sum(up * branch * (1.0 - gate * gate), axis=0, keepdims=True)
    ex_gi.start()
    c_norm.c()
    lg.e()
    total = jnp.zeros((NL, 128), F32)
    for h in range(HL):
        cols = slice(h * HS, (h + 1) * HS)
        total = total + dot(lg.head(h), wk_ref[:, cols], 1, 1) + dot(lg.head(HL + h), wv_ref[:, cols], 1, 1)
    rowi = lax.broadcasted_iota(jnp.int32, (NL, NL), 0)
    coli = lax.broadcasted_iota(jnp.int32, (NL, NL), 1)
    from_row = ((rowi // LR) % NJ) * LI + (rowi // (LR * NJ)) * LR + rowi % LR
    perm = (coli == from_row).astype(F32).astype(BF)
    gl[...] = dot(perm, total.astype(BF), 1, 0).astype(BF).reshape(NI, NJ * LR, 128)
    ex_gl.start()
    ex_gi.wait()
    t = gg_p[...]
    for k in range(1, NI):
        t = t + gg_r[k]
    ggj[...] = t
    ex_gj.start()
    for h in range(HL):
        cols = slice(h * HS, (h + 1) * HS)
        gwk_ref[:, cols] = dot(latt[...], lg.head(h), 1, 0)
        gwv_ref[:, cols] = dot(latt[...], lg.head(HL + h), 1, 0)
    ex_gl.wait()
    t = gl[ia].astype(F32)
    for k in range(1, NI):
        t = t + glr[k].astype(F32)
    wide_r = lax.broadcasted_iota(jnp.int32, (NJ * 16, NJ * LR), 0)
    wide_c = lax.broadcasted_iota(jnp.int32, (NJ * 16, NJ * LR), 1)
    wide = ((wide_r // 16 * LR + wide_r % 16 == wide_c) & (wide_r % 16 < LR)).astype(F32).astype(BF)
    gls[...] = dot(wide, t.astype(BF), 1, 0).astype(BF).reshape(NJ, 16, 128)
    glf[ja] = gls[ja]
    ex_g2.start()
    gst_ref[...] = (up + c_norm.d()).astype(BF)
    ex_go.wait()
    gwo_ref[...] = grad_sum(1).T
    ex_gq.wait()
    gwq_ref[...] = grad_sum(0)
    ex_gj.wait()
    t = ggj[...]
    for k in range(1, NJ):
        t = t + ggj_r[k]
    gg_ref[...] = t
    ex_g2.wait()
    for s in range(NJ):
        glat_ref[:, s * 128 : (s + 1) * 128] = glf[s, 0:LR, :]
    for f in drains:
        f()


def run(sizes, *args):
    NI, NJ, NZ, NX = sizes
    st, lat, wq, wk, wv, wo, gate, img, cnt, up = args
    NA, NR = NZ * NX, NZ * NJ
    TB, DL = st.shape
    WB, WD = wq.shape
    HL = WD // HS
    LR = lat.shape[0]
    LI = NI * LR
    NL = NJ * LI
    LB = NL // NA
    CB = 2 * HL
    TG, DG = NR * TB, NX * WB
    assert CB == NJ and NI == NJ and NZ == 2 and NJ == NZ * NX and DL == NJ * 128 and WB == 128 and TB <= 128
    vm = lambda dt, *s: pltpu.VMEM(s, dt)

    def spread():
        return [
            vm(BF, NJ, TB, WB), vm(BF, NX, NZ, TB, WB), vm(BF, NX, NZ, TB, WB), vm(BF, NI, NX, NZ, TB, WB), vm(BF, TG, DG),
        ]

    def allsum():
        return [
            vm(BF, NX, NZ, CB, LB, 128), vm(BF, NX, NZ, CB, LB, 128), vm(BF, NZ, CB, LB, 128), vm(BF, NR, LB, 128),
            vm(BF, NX, NZ, CB, LB, 128),
        ]

    def ringsum():
        return [vm(BF, NR, TB, WD), vm(BF, NR // 2, TB, WD), vm(BF, NR - 1 - NR // 2, TB, WD), vm(BF, TB, WD)]

    def collect():
        return [
            vm(BF, NI, NX, NZ, TB, WB), vm(BF, NI, NX, NZ, TB, WB), vm(BF, NX, NZ, TB, WB), vm(BF, NX, NZ, TB, WB),
            vm(BF, NJ, TB, WB),
        ]

    scratch = [
        vm(BF, 2, NX, WB, WD), vm(BF, NI, 16, DL), vm(BF, NJ, LI, 128), vm(BF, NJ, LI, 128), vm(BF, 128, NL),
        *spread(), *spread(), *allsum(), *allsum(), *ringsum(), *ringsum(),
        vm(F32, 1, TG), vm(F32, NR, 1, TG), vm(F32, NR, 1, 128), vm(F32, NX, NR, 1, 128),
        vm(BF, NR, TB, WD), vm(BF, NR, TB, WD), vm(F32, NJ, NZ, 1, 128), vm(F32, NI, NZ, 1, 128),
        *collect(), *collect(),
        vm(F32, 1, DL), vm(F32, NI, 1, DL), vm(F32, 1, DL), vm(F32, NJ, 1, DL),
        vm(BF, 2, NX, WB, WD), vm(BF, 2, NX, WB, WD),
        vm(BF, NI, NJ * LR, 128), vm(BF, NI, NJ * LR, 128), vm(BF, NJ, 16, 128), vm(BF, NJ, 16, 128),
        vm(F32, HL, TB, NL), vm(BF, HL, TB, NL),
        pltpu.SemaphoreType.DMA((420,)), pltpu.SemaphoreType.DMA((420,)),
    ]
    v, s = pl.BlockSpec(memory_space=pltpu.VMEM), pl.BlockSpec(memory_space=pltpu.SMEM)
    shape = jax.ShapeDtypeStruct
    out = pl.pallas_call(
        functools.partial(kernel, sizes),
        out_shape=(
            shape((TB, DL), BF), shape((TB, DL), BF), shape((LR, DL), BF), shape((WB, WD), F32),
            shape((WB, WD), F32), shape((WB, WD), F32), shape((WD, WB), F32), shape((1, DL), F32),
        ),
        in_specs=[v] * 8 + [s, v],
        out_specs=tuple([v] * 8),
        scratch_shapes=scratch,
        compiler_params=pltpu.CompilerParams(collective_id=0, has_side_effects=True, vmem_limit_bytes=56 * 2**20),
    )(st, lat, wq, wk, wv, wo, gate.reshape(1, DL), img.reshape(TB, 1), cnt, up)
    return (*out[:7], out[7].reshape(DL))


def solution(mesh, sizes=None):
    if sizes is None:
        sizes = (mesh.shape["ia"], mesh.shape["ja"], 2, mesh.shape["al"] // 2)
    tokens = P(("ja", "ia"), "al")
    weight = P(("al", "ja"), "ia")
    second = P("ia", ("al", "ja"))
    return jax.shard_map(
        functools.partial(run, sizes),
        mesh=mesh,
        in_specs=(tokens, tokens, weight, weight, weight, second, P("al"), P(("ja", "al")), P(), tokens),
        out_specs=(tokens, tokens, tokens, weight, weight, weight, second, P("al")),
        check_vma=False,
    )
```

```python
import functools
import math

import jax
import jax.numpy as jnp
from jax import lax
from jax.experimental import pallas as pl
from jax.experimental.pallas import tpu as pltpu
from jax.sharding import PartitionSpec as P

MESH = pl.DeviceIdType.MESH
D = 8192
EPS = 1e-05
BF = jnp.bfloat16
F32 = jnp.float32
IMGS = 4
HS = 128


def dot(a, b, ca, cb):
    return lax.dot_general(a, b, (((ca,), (cb,)), ((), ())), preferred_element_type=F32)


def loop(lo, hi, f):
    lax.fori_loop(lo, hi, lambda i, c: (f(i), c)[1], 0)


def kernel(sizes, *refs):
    NI, NJ, NZ, NX = sizes
    (
        st_ref, lat_ref, wq_ref, wk_ref, wv_ref, wo_ref, gate_ref, img_ref, cnt_ref, up_ref,
        mixed_ref, gst_ref, glat_ref, gwq_ref, gwk_ref, gwv_ref, gwo_ref, gg_ref,
    ) = refs[:18]
    (
        W, latg, latc, latb, latt,
        s0, s1, s2, s3, strow,
        b0, b1, b2, b3, brrow,
        kv_p, kv_rx, kv_zs, kv_rz, kv_full,
        lg_p, lg_rx, lg_zs, lg_rz, lg_full,
        q_p, q_rr, q_rl, qs,
        a_p, a_rr, a_rl, gs,
        e_p, e_r, im_z, im_x,
        atrow, qgrow, innr, rin,
        outp, outr, out1, out2, out3,
        normp, normr, norm1, norm2, norm3,
        gg_p, gg_r, ggj, ggj_r,
        gp, gpr,
        gl, glr, gls, glf,
        prob, probl,
        ssem, rsem,
    ) = refs[18:]
    NA, NR = NZ * NX, NZ * NJ
    TB, DL = st_ref.shape
    WB, WD = wq_ref.shape
    HL = WD // HS
    LR = lat_ref.shape[0]
    LI = NI * LR
    NL = NJ * LI
    LB = NL // NA
    LAT = NL // IMGS
    CB = 2 * HL
    TG = NR * TB
    DG = NX * WB
    scale = 1.0 / math.sqrt(HS)

    ia, ja, al = lax.axis_index("ia"), lax.axis_index("ja"), lax.axis_index("al")
    x, zh = al % NX, al // NX
    z = zh * NJ + ja
    place = {"ia": (ia, NI), "ja": (ja, NJ), "x": (x, NX), "z": (z, NR)}

    def device(axis, i):
        if axis == "x":
            return {"al": zh * NX + i}
        if axis == "z":
            return {"ja": i % NJ, "al": (i // NJ) * NX + x}
        return {axis: i}

    used = [0]
    drains = []

    def take(n):
        used[0] += n
        assert used[0] <= ssem.shape[0]
        return used[0] - n

    def copy(src, dst, i, dev):
        return pltpu.make_async_remote_copy(
            src_ref=src, dst_ref=dst, send_sem=ssem.at[i], recv_sem=rsem.at[i],
            device_id=dev, device_id_type=MESH,
        )

    class Exchange:
        def __init__(self, axis, src, dst):
            self.axis, self.src, self.dst = axis, src, dst
            self.me, self.n = place[axis]
            self.base = take(self.n)

        def out(self, k):
            peer = (self.me + k) % self.n
            return copy(self.src(peer), self.dst(self.me, k), self.base + k, device(self.axis, peer))

        def into(self, k):
            peer = (self.me - k + self.n) % self.n
            return copy(self.src(peer), self.dst(peer, k), self.base + k, device(self.axis, peer))

        def start(self):
            loop(1, self.n, lambda k: self.out(k).start())
            drains.append(lambda: loop(1, self.n, lambda k: self.out(k).wait_send()))

        def wait(self):
            loop(1, self.n, lambda k: self.into(k).wait_recv())

    HOPS = NR // 4
    ring = {d: device("z", (z + d + NR) % NR) for d in (-2, -1, 1, 2)}

    class RingSum:
        def __init__(self, p, odd, even):
            self.p, self.odd, self.even = p, odd, even
            self.o = {g: take(HOPS) for g in (1, -1)}
            self.e = {g: take(HOPS) for g in (1, -1)}

        def block(self, g, off):
            return self.p.at[(z + g * off + NR) % NR]

        def one(self, g, i, src=None):
            dst = self.odd.at[(1 - g) // 2, i]
            return copy(dst if src is None else src, dst, self.o[g] + i, ring[g])

        def two(self, g, s, src=None):
            dst = self.even.at[(1 - g) // 2, s]
            return copy(dst if src is None else src, dst, self.e[g] + s, ring[2 * g])

        def source(self, g, s):
            if s == 0:
                return self.block(1, 2 * HOPS)
            return self.odd.at[1, 0] if g < 0 and s == 1 else self.even.at[(1 - g) // 2, s - 1]

        def step(self, s):
            if s == 0:
                self.two(1, 0, self.source(1, 0)).start()
                for i in range(HOPS):
                    for g in (1, -1):
                        self.one(g, i, self.block(g, 2 * HOPS - 1 - 2 * i)).start()
                return
            for g in (1, -1):
                self.one(g, s - 1).wait_recv()
                t = self.odd[(1 - g) // 2, s - 1].astype(F32) + self.block(g, 2 * HOPS - 2 * s)[...].astype(F32)
                if g > 0 or s > 1:
                    self.two(g, s - 1).wait_recv()
                    t = t + self.even[(1 - g) // 2, s - 1].astype(F32)
                src = self.source(g, s)
                src[...] = t.astype(BF)
                self.two(g, s, src).start()

        def end(self):
            t = self.p[z].astype(F32)
            for g in (1, -1):
                self.one(g, HOPS - 1).wait_recv()
                self.two(g, HOPS - 1).wait_recv()
                t = t + self.odd[(1 - g) // 2, HOPS - 1].astype(F32) + self.even[(1 - g) // 2, HOPS - 1].astype(F32)

            def drain():
                for s in range(HOPS):
                    for g in (1, -1):
                        self.one(g, s).wait_send()
                        if g > 0 or s > 0:
                            self.two(g, s).wait_send()

            drains.append(drain)
            return t

    class RingGather:
        def __init__(self, buf):
            self.buf = buf
            self.o = {g: take(HOPS) for g in (1, -1)}
            self.e = {g: take(HOPS) for g in (1, -1)}

        def one(self, g, s, frm):
            b = self.buf.at[(z - g * frm + NR) % NR]
            return copy(b, b, self.o[g] + s, ring[g])

        def two(self, g, s, frm):
            b = self.buf.at[(z - g * frm + NR) % NR]
            return copy(b, b, self.e[g] + s, ring[2 * g])

        def step(self, s):
            for g in (1, -1):
                if s > 0:
                    self.two(g, s - 1, 2 * s).wait_recv()
                if g > 0 or s < HOPS - 1:
                    self.two(g, s, 2 * s).start()
                self.one(g, s, 2 * s).start()

        def end(self):
            self.two(1, HOPS - 1, 2 * HOPS).wait_recv()
            for g in (1, -1):
                for s in range(HOPS):
                    self.one(g, s, 2 * s + 1).wait_recv()

            def drain():
                for g in (1, -1):
                    for s in range(HOPS):
                        self.one(g, s, 2 * s).wait_send()
                        if g > 0 or s < HOPS - 1:
                            self.two(g, s, 2 * s).wait_send()

            drains.append(drain)

    class AllSum:
        def __init__(self, p, rx, zs, rz, full):
            self.p, self.rx, self.zs, self.rz, self.full = p, rx, zs, rz, full
            self.x1 = Exchange("x", lambda peer: p.at[peer], lambda s, k: rx.at[k])
            self.z1 = Exchange("z", lambda peer: zs.at[peer // NJ, peer % NJ], lambda s, k: rz.at[k])
            self.z2 = Exchange("z", lambda peer: full.at[x, zh, ja], lambda s, k: full.at[x, s // NJ, s % NJ])
            self.x2 = Exchange("x", lambda peer: full.at[x], lambda s, k: full.at[s])

        def a(self):
            self.x1.start()

        def b(self):
            self.x1.wait()
            t = self.p[x].astype(F32)
            for k in range(1, NX):
                t = t + self.rx[k].astype(F32)
            self.zs[...] = t.astype(BF)
            self.z1.start()

        def c(self):
            self.z1.wait()
            t = self.zs[zh, ja].astype(F32)
            for k in range(1, NR):
                t = t + self.rz[k].astype(F32)
            self.full[x, zh, ja] = t.astype(BF)
            self.z2.start()

        def d(self):
            self.z2.wait()
            self.x2.start()

        def e(self):
            self.x2.wait()

        def head(self, h):
            return jnp.concatenate([self.full[a % NX, a // NX, h] for a in range(NA)], axis=0)

    class Spread:
        def __init__(self, t0, t1, t2, t3, rows):
            self.t0, self.t1, self.t2, self.t3, self.rows = t0, t1, t2, t3, rows
            self.z = Exchange("ja", lambda peer: t0.at[peer], lambda s, k: t1.at[s // NZ, s % NZ])
            self.x = Exchange("x", lambda peer: t1.at[peer], lambda s, k: t2.at[s])
            self.y = Exchange("ia", lambda peer: t3.at[ia], lambda s, k: t3.at[s])

        def load(self, v):
            for s in range(NJ):
                self.t0[s] = v[:, s * WB : (s + 1) * WB]
            self.t1[ja // NZ, ja % NZ] = self.t0[ja]

        def a(self):
            self.z.start()

        def b(self):
            self.z.wait()
            self.x.start()

        def c(self):
            self.x.wait()
            self.t2[x] = self.t1[x]
            self.t3[ia] = self.t2[...]
            self.y.start()

        def d(self):
            self.y.wait()
            for k in range(NX):
                for j in range(NZ):
                    self.rows[j * NI * TB : (j + 1) * NI * TB, k * WB : (k + 1) * WB] = self.t3[:, k, j].reshape(NI * TB, WB)

    class Collect:
        def __init__(self, p, r, t1, t2, t3):
            self.p, self.r, self.t1, self.t2, self.t3 = p, r, t1, t2, t3
            self.y = Exchange("ia", lambda peer: p.at[peer], lambda s, k: r.at[k])
            self.x = Exchange("x", lambda peer: t1.at[peer], lambda s, k: t2.at[s])
            self.z = Exchange("ja", lambda peer: t2.at[peer // NZ, peer % NZ], lambda s, k: t3.at[s])

        def a(self, rows, m):
            for k in range(NX):
                v = dot(rows, W[m, k], 1, 1).astype(BF)
                for j in range(NZ):
                    self.p[:, k, j] = v[j * NI * TB : (j + 1) * NI * TB].reshape(NI, TB, WB)
            self.y.start()

        def b(self, correct=None):
            self.y.wait()
            t = self.p[ia].astype(F32)
            for k in range(1, NI):
                t = t + self.r[k].astype(F32)
            if correct is not None:
                t = correct(t)
            self.t1[...] = t.astype(BF)
            self.t2[x] = self.t1[x]
            self.x.start()

        def c(self):
            self.x.wait()
            self.t3[ja] = self.t2[ja // NZ, ja % NZ]
            self.z.start()

        def d(self):
            self.z.wait()
            return jnp.concatenate([self.t3[s] for s in range(NJ)], axis=1).astype(F32)

    ex_wq = Exchange("x", lambda peer: W.at[0, x], lambda s, k: W.at[0, s])
    ex_wo = Exchange("x", lambda peer: W.at[1, x], lambda s, k: W.at[1, s])
    ex_lat = Exchange("ia", lambda peer: latg.at[ia], lambda s, k: latg.at[s])
    ex_l2 = Exchange("ja", lambda peer: latc.at[peer], lambda s, k: latb.at[s])
    sp_s, sp_b = Spread(s0, s1, s2, s3, strow), Spread(b0, b1, b2, b3, brrow)
    kv = AllSum(kv_p, kv_rx, kv_zs, kv_rz, kv_full)
    lg = AllSum(lg_p, lg_rx, lg_zs, lg_rz, lg_full)
    q_s, a_s = RingSum(q_p, q_rr, q_rl), RingSum(a_p, a_rr, a_rl)
    e_z = Exchange("z", lambda peer: e_p, lambda s, k: e_r.at[k])
    ex_iz = Exchange("z", lambda peer: im_z.at[z], lambda s, k: im_z.at[s])
    ex_ix = Exchange("x", lambda peer: im_x.at[x], lambda s, k: im_x.at[s])
    at_g, qg_g = RingGather(atrow), RingGather(qgrow)
    in_g = Exchange("z", lambda peer: innr.at[ja, zh], lambda s, k: innr.at[s % NJ, s // NJ])
    ex_in = Exchange("ia", lambda peer: innr.at[peer], lambda s, k: rin.at[k])
    c_out, c_norm = Collect(outp, outr, out1, out2, out3), Collect(normp, normr, norm1, norm2, norm3)
    ex_gi = Exchange("ia", lambda peer: gg_p, lambda s, k: gg_r.at[k])
    ex_gj = Exchange("ja", lambda peer: ggj, lambda s, k: ggj_r.at[k])
    ex_gq = Exchange("x", lambda peer: gp.at[0, peer], lambda s, k: gpr.at[0, k])
    ex_go = Exchange("x", lambda peer: gp.at[1, peer], lambda s, k: gpr.at[1, k])
    ex_gl = Exchange("ia", lambda peer: gl.at[peer], lambda s, k: glr.at[k])
    ex_g2 = Exchange("ja", lambda peer: gls.at[peer], lambda s, k: glf.at[s])

    barrier = pltpu.get_barrier_semaphore()
    for axis in ("ia", "x", "z"):
        i, n = place[axis]
        loop(1, n, lambda k: pl.semaphore_signal(barrier, 1, device_id=device(axis, (i + k) % n), device_id_type=MESH))

    lane1 = lax.broadcasted_iota(jnp.int32, (TB, 128), 1)
    sub1 = lax.broadcasted_iota(jnp.int32, (TB, 128), 0)

    def to_row(col):
        return jnp.sum(jnp.where(lane1 == sub1, col, 0.0), axis=0, keepdims=True)

    def to_col(row):
        return jnp.sum(jnp.where(lane1 == sub1, row, 0.0), axis=1, keepdims=True)

    sp_s.load(st_ref[...])
    latg[ia] = jnp.zeros((16, DL), BF)
    latg[ia, 0:LR, :] = lat_ref[...]
    W[0, x] = wq_ref[...]
    gate = jnp.tanh(gate_ref[...])
    sp_b.load((up_ref[...].astype(F32) * gate).astype(BF))
    im_z[z] = jnp.zeros((1, 128), F32)
    im_z[z, :, 0:TB] = img_ref[...].astype(F32)
    pl.semaphore_wait(barrier, NI - 1 + NX - 1 + NR - 1)

    sp_s.a()
    ex_lat.start()
    sp_b.a()
    ex_iz.start()
    W[1, x] = wo_ref[...].T

    sp_s.b()
    ex_wq.start()
    ex_lat.wait()
    pick_r = lax.broadcasted_iota(jnp.int32, (LI, NI * 16), 0)
    pick_c = lax.broadcasted_iota(jnp.int32, (LI, NI * 16), 1)
    pick = (pick_c == (pick_r // LR) * 16 + pick_r % LR).astype(F32).astype(BF)
    packed = dot(pick, latg[...].reshape(NI * 16, DL), 1, 0).astype(BF)
    for s in range(NJ):
        latc[s] = packed[:, s * 128 : (s + 1) * 128]
    latb[ja] = latc[ja]
    ex_l2.start()
    sp_s.c()
    sp_b.b()
    ex_iz.wait()
    im_x[x] = im_z[...]
    ex_ix.start()

    ex_l2.wait()
    lat = latb[...].reshape(NL, 128)
    latt[...] = lat.T
    for h in range(CB):
        wref = wk_ref if h < HL else wv_ref
        c = h % HL
        part = dot(lat, wref[:, c * HS : (c + 1) * HS], 1, 0).astype(BF)
        for a in range(NA):
            kv_p[a % NX, a // NX, h] = part[a * LB : (a + 1) * LB]
    kv.a()
    sp_b.c()
    ex_wo.start()

    def rows_times(rows, m, p):
        acc = dot(rows, W[m].reshape(DG, WD), 1, 0).astype(BF)
        for d in range(NR):
            p[d] = acc[d * TB : (d + 1) * TB]

    sp_s.d()
    ex_wq.wait()
    rows_times(strow[...], 0, q_p)
    q_s.step(0)
    sq = strow[...].astype(F32)
    sq = (sq * sq).astype(BF)
    e_p[...] = dot(jnp.ones((8, DG), BF), sq, 1, 1)[0:1]
    e_z.start()
    kv.b()
    q_s.step(1)
    for s in range(2, HOPS):
        q_s.step(s)
    kv.c()
    sp_b.d()
    ex_wo.wait()
    rows_times(brrow[...], 1, a_p)
    a_s.step(0)
    kv.d()
    e_z.wait()
    energy = e_p[...]
    for k in range(1, NR):
        energy = energy + e_r[k]
    inv_row = lax.rsqrt(energy / D + EPS)
    lane = lax.broadcasted_iota(jnp.int32, (TB, TG), 1)
    sub = lax.broadcasted_iota(jnp.int32, (TB, TG), 0)

    def column(block):
        return jnp.sum(jnp.where(lane == block * TB + sub, inv_row, 0.0), axis=1, keepdims=True)

    inv_attn = column(z)
    ex_ix.wait()
    image_col = to_col(im_x[ja % NX, (ja // NX) * NJ + NZ * x + zh])
    slot = lax.broadcasted_iota(jnp.int32, (TB, NL), 1)
    image = slot // LAT
    count = jnp.where(image == 0, cnt_ref[0], jnp.where(image == 1, cnt_ref[1], jnp.where(image == 2, cnt_ref[2], cnt_ref[3])))
    allowed = (image_col == image.astype(F32)) & (slot % LAT < count)
    q = q_s.end() * inv_attn
    qs[...] = q.astype(BF)
    a_s.step(1)
    kv.e()
    for s in range(2, HOPS - 1):
        a_s.step(s)
    for h in range(HL):
        cols = slice(h * HS, (h + 1) * HS)
        sco = dot(qs[:, cols], kv.head(h), 1, 1) * scale
        raised = jnp.where(allowed, jnp.exp(sco), 0.0)
        pr = raised / jnp.sum(raised, axis=1, keepdims=True)
        prob[h] = pr
        probl[h] = pr.astype(BF)
        atrow[z, :, cols] = dot(probl[h], kv.head(HL + h), 1, 0).astype(BF)
    at_g.step(0)
    if HOPS > 2:
        a_s.step(HOPS - 1)
    at_g.step(1)
    gs[...] = a_s.end().astype(BF)
    inner = jnp.zeros((TB, 1), F32)
    for h in range(HL):
        cols = slice(h * HS, (h + 1) * HS)
        kh = kv.head(h)
        gh = gs[:, cols]
        qh = qs[:, cols]
        pg = dot(gh, kv.head(HL + h), 1, 1)
        pr = prob[h]
        sg = pr * (pg - jnp.sum(pr * pg, axis=1, keepdims=True))
        sl = sg.astype(BF)
        qg = dot(sl, kh, 1, 0) * scale * inv_attn
        inner = inner + jnp.sum(qg * qh.astype(F32), axis=1, keepdims=True)
        qgrow[z, :, cols] = qg.astype(BF)
        kt = (dot(sl, qh, 0, 0) * scale).astype(BF)
        vt = dot(probl[h], gh, 0, 0).astype(BF)
        for a in range(NA):
            lg_p[a % NX, a // NX, h] = kt[a * LB : (a + 1) * LB]
            lg_p[a % NX, a // NX, HL + h] = vt[a * LB : (a + 1) * LB]
    qg_g.step(0)
    innr[ja, zh] = to_row(inner)
    in_g.start()
    lg.a()
    qg_g.step(1)
    for s in range(2, HOPS):
        at_g.step(s)
        qg_g.step(s)
    at_g.end()

    def grad_parts(left_rows, right_rows, m):
        for k in range(NX):
            gp[m, k] = dot(left_rows[:, k * WB : (k + 1) * WB], right_rows, 0, 0).astype(BF)

    def grad_sum(m):
        t = gp[m, x].astype(F32)
        for k in range(1, NX):
            t = t + gpr[m, k].astype(F32)
        return t

    attn_rows = atrow[...].reshape(TG, WD)
    c_out.a(attn_rows, 1)
    lg.b()
    in_g.wait()
    ex_in.start()
    qg_g.end()
    qg_rows = qgrow[...].reshape(TG, WD)
    c_norm.a(qg_rows, 0)
    lg.c()
    grad_parts(brrow[...], attn_rows, 1)
    ex_go.start()
    c_out.b()
    grad_parts(strow[...], qg_rows, 0)
    ex_gq.start()
    lg.d()
    c_out.c()

    def correct(t):
        ex_in.wait()
        own = innr[ia]
        for k in range(1, NI):
            own = own + rin[k]
        parts = []
        for j in range(NZ):
            coef = column(j * NI + ia) * to_col(own[j]) / D
            parts.append(t[:, j] - s2[:, j].astype(F32) * coef[None])
        return jnp.stack(parts, axis=1)

    c_norm.b(correct)
    up = up_ref[...].astype(F32)
    branch = c_out.d()
    mixed_ref[...] = (st_ref[...].astype(F32) + gate * branch).astype(BF)
    gg_p[...] = jnp.sum(up * branch * (1.0 - gate * gate), axis=0, keepdims=True)
    ex_gi.start()
    c_norm.c()
    lg.e()
    total = jnp.zeros((NL, 128), F32)
    for h in range(HL):
        cols = slice(h * HS, (h + 1) * HS)
        total = total + dot(lg.head(h), wk_ref[:, cols], 1, 1) + dot(lg.head(HL + h), wv_ref[:, cols], 1, 1)
    rowi = lax.broadcasted_iota(jnp.int32, (NL, NL), 0)
    coli = lax.broadcasted_iota(jnp.int32, (NL, NL), 1)
    from_row = ((rowi // LR) % NJ) * LI + (rowi // (LR * NJ)) * LR + rowi % LR
    perm = (coli == from_row).astype(F32).astype(BF)
    gl[...] = dot(perm, total.astype(BF), 1, 0).astype(BF).reshape(NI, NJ * LR, 128)
    ex_gl.start()
    ex_gi.wait()
    t = gg_p[...]
    for k in range(1, NI):
        t = t + gg_r[k]
    ggj[...] = t
    ex_gj.start()
    for h in range(HL):
        cols = slice(h * HS, (h + 1) * HS)
        gwk_ref[:, cols] = dot(latt[...], lg.head(h), 1, 0).astype(BF)
        gwv_ref[:, cols] = dot(latt[...], lg.head(HL + h), 1, 0).astype(BF)
    ex_gl.wait()
    t = gl[ia].astype(F32)
    for k in range(1, NI):
        t = t + glr[k].astype(F32)
    wide_r = lax.broadcasted_iota(jnp.int32, (NJ * 16, NJ * LR), 0)
    wide_c = lax.broadcasted_iota(jnp.int32, (NJ * 16, NJ * LR), 1)
    wide = ((wide_r // 16 * LR + wide_r % 16 == wide_c) & (wide_r % 16 < LR)).astype(F32).astype(BF)
    gls[...] = dot(wide, t.astype(BF), 1, 0).astype(BF).reshape(NJ, 16, 128)
    glf[ja] = gls[ja]
    ex_g2.start()
    gst_ref[...] = (up + c_norm.d()).astype(BF)
    ex_go.wait()
    gwo_ref[...] = grad_sum(1).astype(BF)
    ex_gq.wait()
    gwq_ref[...] = grad_sum(0).astype(BF)
    ex_gj.wait()
    t = ggj[...]
    for k in range(1, NJ):
        t = t + ggj_r[k]
    gg_ref[...] = t
    ex_g2.wait()
    for s in range(NJ):
        glat_ref[:, s * 128 : (s + 1) * 128] = glf[s, 0:LR, :]
    for f in drains:
        f()


def finish(*refs):
    for i in range(8):
        v = refs[i][...].astype(refs[8 + i].dtype)
        refs[8 + i][...] = v.T if i == 6 else v


def run(sizes, *args):
    NI, NJ, NZ, NX = sizes
    st, lat, wq, wk, wv, wo, gate, img, cnt, up = args
    NA, NR = NZ * NX, NZ * NJ
    TB, DL = st.shape
    WB, WD = wq.shape
    HL = WD // HS
    LR = lat.shape[0]
    LI = NI * LR
    NL = NJ * LI
    LB = NL // NA
    CB = 2 * HL
    TG, DG = NR * TB, NX * WB
    assert CB == NJ and NI == NJ and NZ == 2 and NJ == NZ * NX and DL == NJ * 128 and WB == 128 and TB <= 128
    vm = lambda dt, *s: pltpu.VMEM(s, dt)

    def spread():
        return [
            vm(BF, NJ, TB, WB), vm(BF, NX, NZ, TB, WB), vm(BF, NX, NZ, TB, WB), vm(BF, NI, NX, NZ, TB, WB), vm(BF, TG, DG),
        ]

    def allsum():
        return [
            vm(BF, NX, NZ, CB, LB, 128), vm(BF, NX, NZ, CB, LB, 128), vm(BF, NZ, CB, LB, 128), vm(BF, NR, LB, 128),
            vm(BF, NX, NZ, CB, LB, 128),
        ]

    def ringsum():
        return [vm(BF, NR, TB, WD), vm(BF, 2, NR // 4, TB, WD), vm(BF, 2, NR // 4, TB, WD), vm(BF, TB, WD)]

    def collect():
        return [
            vm(BF, NI, NX, NZ, TB, WB), vm(BF, NI, NX, NZ, TB, WB), vm(BF, NX, NZ, TB, WB), vm(BF, NX, NZ, TB, WB),
            vm(BF, NJ, TB, WB),
        ]

    scratch = [
        vm(BF, 2, NX, WB, WD), vm(BF, NI, 16, DL), vm(BF, NJ, LI, 128), vm(BF, NJ, LI, 128), vm(BF, 128, NL),
        *spread(), *spread(), *allsum(), *allsum(), *ringsum(), *ringsum(),
        vm(F32, 1, TG), vm(F32, NR, 1, TG), vm(F32, NR, 1, 128), vm(F32, NX, NR, 1, 128),
        vm(BF, NR, TB, WD), vm(BF, NR, TB, WD), vm(F32, NJ, NZ, 1, 128), vm(F32, NI, NZ, 1, 128),
        *collect(), *collect(),
        vm(F32, 1, DL), vm(F32, NI, 1, DL), vm(F32, 1, DL), vm(F32, NJ, 1, DL),
        vm(BF, 2, NX, WB, WD), vm(BF, 2, NX, WB, WD),
        vm(BF, NI, NJ * LR, 128), vm(BF, NI, NJ * LR, 128), vm(BF, NJ, 16, 128), vm(BF, NJ, 16, 128),
        vm(F32, HL, TB, NL), vm(BF, HL, TB, NL),
        pltpu.SemaphoreType.DMA((420,)), pltpu.SemaphoreType.DMA((420,)),
    ]
    v, s = pl.BlockSpec(memory_space=pltpu.VMEM), pl.BlockSpec(memory_space=pltpu.SMEM)
    shape = jax.ShapeDtypeStruct
    out = pl.pallas_call(
        functools.partial(kernel, sizes),
        out_shape=(
            shape((TB, DL), BF), shape((TB, DL), BF), shape((LR, DL), BF), shape((WB, WD), BF),
            shape((WB, WD), BF), shape((WB, WD), BF), shape((WB, WD), BF), shape((1, DL), F32),
        ),
        in_specs=[v] * 8 + [s, v],
        out_specs=tuple([v] * 8),
        scratch_shapes=scratch,
        compiler_params=pltpu.CompilerParams(collective_id=0, has_side_effects=True, vmem_limit_bytes=56 * 2**20),
    )(st, lat, wq, wk, wv, wo, gate.reshape(1, DL), img.reshape(1, TB), cnt, up)
    out = pl.pallas_call(
        finish,
        out_shape=(
            shape((TB, DL), BF), shape((TB, DL), BF), shape((LR, DL), BF), shape((WB, WD), F32),
            shape((WB, WD), F32), shape((WB, WD), F32), shape((WD, WB), F32), shape((1, DL), F32),
        ),
        in_specs=[v] * 8,
        out_specs=tuple([v] * 8),
    )(*out)
    return (*out[:7], out[7].reshape(DL))


def solution(mesh, sizes=None):
    if sizes is None:
        sizes = (mesh.shape["ia"], mesh.shape["ja"], 2, mesh.shape["al"] // 2)
    tokens = P(("ja", "ia"), "al")
    weight = P(("al", "ja"), "ia")
    second = P("ia", ("al", "ja"))
    return jax.shard_map(
        functools.partial(run, sizes),
        mesh=mesh,
        in_specs=(tokens, tokens, weight, weight, weight, second, P("al"), P(("ja", "al")), P(), tokens),
        out_specs=(tokens, tokens, tokens, weight, weight, weight, second, P("al")),
        check_vma=False,
    )
```

```python
import functools
import math

import jax
import jax.numpy as jnp
from jax import lax
from jax.experimental import pallas as pl
from jax.experimental.pallas import tpu as pltpu
from jax.sharding import PartitionSpec as P

MESH = pl.DeviceIdType.MESH
D = 8192
EPS = 1e-05
BF = jnp.bfloat16
F32 = jnp.float32
IMGS = 4
HS = 128


def dot(a, b, ca, cb):
    return lax.dot_general(a, b, (((ca,), (cb,)), ((), ())), preferred_element_type=F32)


def loop(lo, hi, f):
    lax.fori_loop(lo, hi, lambda i, c: (f(i), c)[1], 0)


def kernel(sizes, *refs):
    NI, NJ, NZ, NX = sizes
    (
        st_ref, lat_ref, wq_ref, wk_ref, wv_ref, wo_ref, gate_ref, img_ref, cnt_ref, up_ref,
        mixed_ref, gst_ref, glat_ref, gwq_ref, gwk_ref, gwv_ref, gwo_ref, gg_ref,
    ) = refs[:18]
    (
        W, latg, latc, latb, latt,
        s0, s1, s2, s3, strow,
        b0, b1, b2, b3, brrow,
        kv_p, kv_rx, kv_zs, kv_rz, kv_full,
        lg_p, lg_rx, lg_zs, lg_rz, lg_full,
        q_p, q_rr, q_rl, qs,
        a_p, a_rr, a_rl, gs,
        e_p, e_r, im_z, im_x,
        atrow, qgrow, innr, rin,
        outp, outr, out1, out2, out3,
        normp, normr, norm1, norm2, norm3,
        gg_p, gg_r, ggj, ggj_r,
        gp, gpr,
        gl, glr, gls, glf,
        prob, probl,
        ssem, rsem,
    ) = refs[18:]
    NA, NR = NZ * NX, NZ * NJ
    TB, DL = st_ref.shape
    WB, WD = wq_ref.shape
    HL = WD // HS
    LR = lat_ref.shape[0]
    LI = NI * LR
    NL = NJ * LI
    LB = NL // NA
    LAT = NL // IMGS
    CB = 2 * HL
    TG = NR * TB
    DG = NX * WB
    scale = 1.0 / math.sqrt(HS)

    ia, ja, al = lax.axis_index("ia"), lax.axis_index("ja"), lax.axis_index("al")
    x, zh = lax.rem(al, NX), lax.div(al, NX)
    z = zh * NJ + ja
    place = {"ia": (ia, NI), "ja": (ja, NJ), "x": (x, NX), "z": (z, NR)}

    def device(axis, i):
        if axis == "x":
            return {"al": zh * NX + i}
        if axis == "z":
            return {"ja": lax.rem(i, NJ), "al": lax.div(i, NJ) * NX + x}
        return {axis: i}

    used = [0]
    drains = []
    seen = [0]

    def settle():
        for f in drains[: seen[0]]:
            f()
        del drains[: seen[0]]
        seen[0] = len(drains)


    def take(n):
        used[0] += n
        assert used[0] <= ssem.shape[0]
        return used[0] - n

    def copy(src, dst, i, dev):
        return pltpu.make_async_remote_copy(
            src_ref=src, dst_ref=dst, send_sem=ssem.at[i], recv_sem=rsem.at[i],
            device_id=dev, device_id_type=MESH,
        )

    class Exchange:
        def __init__(self, axis, src, dst):
            self.axis, self.src, self.dst = axis, src, dst
            self.me, self.n = place[axis]
            self.base = take(self.n)

        def out(self, k):
            peer = lax.rem(self.me + k, self.n)
            return copy(self.src(peer), self.dst(self.me, k), self.base + k, device(self.axis, peer))

        def into(self, k):
            peer = lax.rem(self.me - k + self.n, self.n)
            return copy(self.src(peer), self.dst(peer, k), self.base + k, device(self.axis, peer))

        def start(self):
            loop(1, self.n, lambda k: self.out(k).start())
            drains.append(lambda: loop(1, self.n, lambda k: self.out(k).wait_send()))

        def wait(self):
            loop(1, self.n, lambda k: self.into(k).wait_recv())

    HOPS = NR // 4
    ring = {d: device("z", lax.rem(z + d + NR, NR)) for d in (-2, -1, 1, 2)}

    class RingSum:
        def __init__(self, p, odd, even):
            self.p, self.odd, self.even = p, odd, even
            self.o = {g: take(HOPS) for g in (1, -1)}
            self.e = {g: take(HOPS) for g in (1, -1)}

        def block(self, g, off):
            return self.p.at[lax.rem(z + g * off + NR, NR)]

        def one(self, g, i, src=None):
            dst = self.odd.at[(1 - g) // 2, i]
            return copy(dst if src is None else src, dst, self.o[g] + i, ring[g])

        def two(self, g, s, src=None):
            dst = self.even.at[(1 - g) // 2, s]
            return copy(dst if src is None else src, dst, self.e[g] + s, ring[2 * g])

        def source(self, g, s):
            if s == 0:
                return self.block(1, 2 * HOPS)
            return self.odd.at[1, 0] if g < 0 and s == 1 else self.even.at[(1 - g) // 2, s - 1]

        def step(self, s):
            if s == 0:
                self.two(1, 0, self.source(1, 0)).start()
                for i in range(HOPS):
                    for g in (1, -1):
                        self.one(g, i, self.block(g, 2 * HOPS - 1 - 2 * i)).start()
                return
            for g in (1, -1):
                self.one(g, s - 1).wait_recv()
                t = self.odd[(1 - g) // 2, s - 1].astype(F32) + self.block(g, 2 * HOPS - 2 * s)[...].astype(F32)
                if g > 0 or s > 1:
                    self.two(g, s - 1).wait_recv()
                    t = t + self.even[(1 - g) // 2, s - 1].astype(F32)
                src = self.source(g, s)
                src[...] = t.astype(BF)
                self.two(g, s, src).start()

        def end(self):
            t = self.p[z].astype(F32)
            for g in (1, -1):
                self.one(g, HOPS - 1).wait_recv()
                self.two(g, HOPS - 1).wait_recv()
                t = t + self.odd[(1 - g) // 2, HOPS - 1].astype(F32) + self.even[(1 - g) // 2, HOPS - 1].astype(F32)

            def drain():
                for s in range(HOPS):
                    for g in (1, -1):
                        self.one(g, s).wait_send()
                        if g > 0 or s > 0:
                            self.two(g, s).wait_send()

            drains.append(drain)
            return t

    class RingGather:
        def __init__(self, buf):
            self.buf = buf
            self.o = {g: take(HOPS) for g in (1, -1)}
            self.e = {g: take(HOPS) for g in (1, -1)}

        def one(self, g, s, frm):
            b = self.buf.at[lax.rem(z - g * frm + NR, NR)]
            return copy(b, b, self.o[g] + s, ring[g])

        def two(self, g, s, frm):
            b = self.buf.at[lax.rem(z - g * frm + NR, NR)]
            return copy(b, b, self.e[g] + s, ring[2 * g])

        def step(self, s):
            for g in (1, -1):
                if s > 0:
                    self.two(g, s - 1, 2 * s).wait_recv()
                if g > 0 or s < HOPS - 1:
                    self.two(g, s, 2 * s).start()
                self.one(g, s, 2 * s).start()

        def end(self):
            self.two(1, HOPS - 1, 2 * HOPS).wait_recv()
            for g in (1, -1):
                for s in range(HOPS):
                    self.one(g, s, 2 * s + 1).wait_recv()

            def drain():
                for g in (1, -1):
                    for s in range(HOPS):
                        self.one(g, s, 2 * s).wait_send()
                        if g > 0 or s < HOPS - 1:
                            self.two(g, s, 2 * s).wait_send()

            drains.append(drain)

    class AllSum:
        def __init__(self, p, rx, zs, rz, full):
            self.p, self.rx, self.zs, self.rz, self.full = p, rx, zs, rz, full
            self.x1 = Exchange("x", lambda peer: p.at[peer], lambda s, k: rx.at[k])
            self.z1 = Exchange("z", lambda peer: zs.at[lax.div(peer, NJ), lax.rem(peer, NJ)], lambda s, k: rz.at[k])
            self.z2 = Exchange("z", lambda peer: full.at[x, zh, ja], lambda s, k: full.at[x, lax.div(s, NJ), lax.rem(s, NJ)])
            self.x2 = Exchange("x", lambda peer: full.at[x], lambda s, k: full.at[s])

        def a(self):
            self.x1.start()

        def b(self):
            self.x1.wait()
            t = self.p[x].astype(F32)
            for k in range(1, NX):
                t = t + self.rx[k].astype(F32)
            self.zs[...] = t.astype(BF)
            self.z1.start()

        def c(self):
            self.z1.wait()
            t = self.zs[zh, ja].astype(F32)
            for k in range(1, NR):
                t = t + self.rz[k].astype(F32)
            self.full[x, zh, ja] = t.astype(BF)
            self.z2.start()

        def d(self):
            self.z2.wait()
            self.x2.start()

        def e(self):
            self.x2.wait()

        def head(self, h):
            return jnp.concatenate([self.full[a % NX, a // NX, h] for a in range(NA)], axis=0)

    class Spread:
        def __init__(self, t0, t1, t2, t3, rows):
            self.t0, self.t1, self.t2, self.t3, self.rows = t0, t1, t2, t3, rows
            self.z = Exchange("ja", lambda peer: t0.at[peer], lambda s, k: t1.at[lax.div(s, NZ), lax.rem(s, NZ)])
            self.x = Exchange("x", lambda peer: t1.at[peer], lambda s, k: t2.at[s])
            self.y = Exchange("ia", lambda peer: t3.at[ia], lambda s, k: t3.at[s])

        def load(self, v):
            for s in range(NJ):
                self.t0[s] = v[:, s * WB : (s + 1) * WB]
            self.t1[ja // NZ, ja % NZ] = self.t0[ja]

        def a(self):
            self.z.start()

        def b(self):
            self.z.wait()
            self.x.start()

        def c(self):
            self.x.wait()
            self.t2[x] = self.t1[x]
            self.t3[ia] = self.t2[...]
            self.y.start()

        def d(self):
            self.y.wait()
            for k in range(NX):
                for j in range(NZ):
                    self.rows[j * NI * TB : (j + 1) * NI * TB, k * WB : (k + 1) * WB] = self.t3[:, k, j].reshape(NI * TB, WB)

    class Collect:
        def __init__(self, p, r, t1, t2, t3):
            self.p, self.r, self.t1, self.t2, self.t3 = p, r, t1, t2, t3
            self.y = Exchange("ia", lambda peer: p.at[peer], lambda s, k: r.at[k])
            self.x = Exchange("x", lambda peer: t1.at[peer], lambda s, k: t2.at[s])
            self.z = Exchange("ja", lambda peer: t2.at[lax.div(peer, NZ), lax.rem(peer, NZ)], lambda s, k: t3.at[s])

        def a(self, rows, m):
            for k in range(NX):
                v = dot(rows, W[m, k], 1, 1).astype(BF)
                for j in range(NZ):
                    self.p[:, k, j] = v[j * NI * TB : (j + 1) * NI * TB].reshape(NI, TB, WB)
            self.y.start()

        def b(self, correct=None):
            self.y.wait()
            t = self.p[ia].astype(F32)
            for k in range(1, NI):
                t = t + self.r[k].astype(F32)
            if correct is not None:
                t = correct(t)
            self.t1[...] = t.astype(BF)
            self.t2[x] = self.t1[x]
            self.x.start()

        def c(self):
            self.x.wait()
            self.t3[ja] = self.t2[ja // NZ, ja % NZ]
            self.z.start()

        def d(self):
            self.z.wait()
            return jnp.concatenate([self.t3[s] for s in range(NJ)], axis=1).astype(F32)

    ex_wq = Exchange("x", lambda peer: W.at[0, x], lambda s, k: W.at[0, s])
    ex_wo = Exchange("x", lambda peer: W.at[1, x], lambda s, k: W.at[1, s])
    ex_lat = Exchange("ia", lambda peer: latg.at[ia], lambda s, k: latg.at[s])
    ex_l2 = Exchange("ja", lambda peer: latc.at[peer], lambda s, k: latb.at[s])
    sp_s, sp_b = Spread(s0, s1, s2, s3, strow), Spread(b0, b1, b2, b3, brrow)
    kv = AllSum(kv_p, kv_rx, kv_zs, kv_rz, kv_full)
    lg = AllSum(lg_p, lg_rx, lg_zs, lg_rz, lg_full)
    q_s, a_s = RingSum(q_p, q_rr, q_rl), RingSum(a_p, a_rr, a_rl)
    e_z = Exchange("z", lambda peer: e_p, lambda s, k: e_r.at[k])
    ex_iz = Exchange("z", lambda peer: im_z.at[z], lambda s, k: im_z.at[s])
    ex_ix = Exchange("x", lambda peer: im_x.at[x], lambda s, k: im_x.at[s])
    at_g, qg_g = RingGather(atrow), RingGather(qgrow)
    in_g = Exchange("z", lambda peer: innr.at[ja, zh], lambda s, k: innr.at[lax.rem(s, NJ), lax.div(s, NJ)])
    ex_in = Exchange("ia", lambda peer: innr.at[peer], lambda s, k: rin.at[k])
    c_out, c_norm = Collect(outp, outr, out1, out2, out3), Collect(normp, normr, norm1, norm2, norm3)
    ex_gi = Exchange("ia", lambda peer: gg_p, lambda s, k: gg_r.at[k])
    ex_gj = Exchange("ja", lambda peer: ggj, lambda s, k: ggj_r.at[k])
    ex_gq = Exchange("x", lambda peer: gp.at[0, peer], lambda s, k: gpr.at[0, k])
    ex_go = Exchange("x", lambda peer: gp.at[1, peer], lambda s, k: gpr.at[1, k])
    ex_gl = Exchange("ia", lambda peer: gl.at[peer], lambda s, k: glr.at[k])
    ex_g2 = Exchange("ja", lambda peer: gls.at[peer], lambda s, k: glf.at[s])

    barrier = pltpu.get_barrier_semaphore()
    for axis in ("ia", "x", "z"):
        i, n = place[axis]
        loop(1, n, lambda k: pl.semaphore_signal(barrier, 1, device_id=device(axis, lax.rem(i + k, n)), device_id_type=MESH))

    lane1 = lax.broadcasted_iota(jnp.int32, (TB, 128), 1)
    sub1 = lax.broadcasted_iota(jnp.int32, (TB, 128), 0)

    def to_row(col):
        return jnp.sum(jnp.where(lane1 == sub1, col, 0.0), axis=0, keepdims=True)

    def to_col(row):
        return jnp.sum(jnp.where(lane1 == sub1, row, 0.0), axis=1, keepdims=True)

    sp_s.load(st_ref[...])
    latg[ia] = jnp.zeros((16, DL), BF)
    latg[ia, 0:LR, :] = lat_ref[...]
    W[0, x] = wq_ref[...]
    gate = jnp.tanh(gate_ref[...])
    sp_b.load((up_ref[...].astype(F32) * gate).astype(BF))
    im_z[z] = jnp.zeros((1, 128), F32)
    im_z[z, :, 0:TB] = img_ref[...].astype(F32)
    pl.semaphore_wait(barrier, NI - 1 + NX - 1 + NR - 1)

    sp_s.a()
    ex_lat.start()
    sp_b.a()
    ex_iz.start()
    W[1, x] = wo_ref[...].T

    sp_s.b()
    ex_wq.start()
    ex_lat.wait()
    pick_r = lax.broadcasted_iota(jnp.int32, (LI, NI * 16), 0)
    pick_c = lax.broadcasted_iota(jnp.int32, (LI, NI * 16), 1)
    pick = (pick_c == (pick_r // LR) * 16 + pick_r % LR).astype(F32).astype(BF)
    packed = dot(pick, latg[...].reshape(NI * 16, DL), 1, 0).astype(BF)
    for s in range(NJ):
        latc[s] = packed[:, s * 128 : (s + 1) * 128]
    latb[ja] = latc[ja]
    ex_l2.start()
    sp_s.c()
    sp_b.b()
    ex_iz.wait()
    im_x[x] = im_z[...]
    ex_ix.start()

    settle()
    ex_l2.wait()
    lat = latb[...].reshape(NL, 128)
    latt[...] = lat.T
    for h in range(CB):
        wref = wk_ref if h < HL else wv_ref
        c = h % HL
        part = dot(lat, wref[:, c * HS : (c + 1) * HS], 1, 0).astype(BF)
        for a in range(NA):
            kv_p[a % NX, a // NX, h] = part[a * LB : (a + 1) * LB]
    kv.a()
    sp_b.c()
    ex_wo.start()

    def rows_times(rows, m, p):
        acc = dot(rows, W[m].reshape(DG, WD), 1, 0).astype(BF)
        for d in range(NR):
            p[d] = acc[d * TB : (d + 1) * TB]

    settle()
    sp_s.d()
    ex_wq.wait()
    rows_times(strow[...], 0, q_p)
    q_s.step(0)
    sq = strow[...].astype(F32)
    sq = (sq * sq).astype(BF)
    e_p[...] = dot(jnp.ones((8, DG), BF), sq, 1, 1)[0:1]
    e_z.start()
    kv.b()
    settle()
    sp_b.d()
    ex_wo.wait()
    rows_times(brrow[...], 1, a_p)
    a_s.step(0)
    q_s.step(1)
    a_s.step(1)
    kv.c()
    for s in range(2, HOPS):
        settle()
        q_s.step(s)
        a_s.step(s)
    kv.d()
    e_z.wait()
    energy = e_p[...]
    for k in range(1, NR):
        energy = energy + e_r[k]
    inv_row = lax.rsqrt(energy / D + EPS)
    lane = lax.broadcasted_iota(jnp.int32, (TB, TG), 1)
    sub = lax.broadcasted_iota(jnp.int32, (TB, TG), 0)

    def column(block):
        return jnp.sum(jnp.where(lane == block * TB + sub, inv_row, 0.0), axis=1, keepdims=True)

    inv_attn = column(z)
    ex_ix.wait()
    image_col = to_col(im_x[ja % NX, (ja // NX) * NJ + NZ * x + zh])
    slot = lax.broadcasted_iota(jnp.int32, (TB, NL), 1)
    image = slot // LAT
    count = jnp.where(image == 0, cnt_ref[0], jnp.where(image == 1, cnt_ref[1], jnp.where(image == 2, cnt_ref[2], cnt_ref[3])))
    allowed = (image_col == image.astype(F32)) & (slot % LAT < count)
    q = q_s.end() * inv_attn
    qs[...] = q.astype(BF)
    gs[...] = a_s.end().astype(BF)
    settle()
    kv.e()
    for h in range(HL):
        cols = slice(h * HS, (h + 1) * HS)
        sco = dot(qs[:, cols], kv.head(h), 1, 1) * scale
        raised = jnp.where(allowed, jnp.exp(sco), 0.0)
        pr = raised / jnp.sum(raised, axis=1, keepdims=True)
        prob[h] = pr
        probl[h] = pr.astype(BF)
        atrow[z, :, cols] = dot(probl[h], kv.head(HL + h), 1, 0).astype(BF)
    at_g.step(0)
    inner = jnp.zeros((TB, 1), F32)
    for h in range(HL):
        cols = slice(h * HS, (h + 1) * HS)
        kh = kv.head(h)
        gh = gs[:, cols]
        qh = qs[:, cols]
        pg = dot(gh, kv.head(HL + h), 1, 1)
        pr = prob[h]
        sg = pr * (pg - jnp.sum(pr * pg, axis=1, keepdims=True))
        sl = sg.astype(BF)
        qg = dot(sl, kh, 1, 0) * scale * inv_attn
        inner = inner + jnp.sum(qg * qh.astype(F32), axis=1, keepdims=True)
        qgrow[z, :, cols] = qg.astype(BF)
        kt = (dot(sl, qh, 0, 0) * scale).astype(BF)
        vt = dot(probl[h], gh, 0, 0).astype(BF)
        for a in range(NA):
            lg_p[a % NX, a // NX, h] = kt[a * LB : (a + 1) * LB]
            lg_p[a % NX, a // NX, HL + h] = vt[a * LB : (a + 1) * LB]
    qg_g.step(0)
    lg.a()
    innr[ja, zh] = to_row(inner)
    in_g.start()
    at_g.step(1)
    qg_g.step(1)
    lg.b()
    for s in range(2, HOPS):
        settle()
        at_g.step(s)
        qg_g.step(s)

    def grad_parts(left_rows, right_rows, m):
        for k in range(NX):
            gp[m, k] = dot(left_rows[:, k * WB : (k + 1) * WB], right_rows, 0, 0).astype(BF)

    def grad_sum(m):
        t = gp[m, x].astype(F32)
        for k in range(1, NX):
            t = t + gpr[m, k].astype(F32)
        return t

    at_g.end()
    attn_rows = atrow[...].reshape(TG, WD)
    c_out.a(attn_rows, 1)
    qg_g.end()
    qg_rows = qgrow[...].reshape(TG, WD)
    c_norm.a(qg_rows, 0)
    lg.c()
    in_g.wait()
    ex_in.start()
    grad_parts(brrow[...], attn_rows, 1)
    ex_go.start()
    settle()
    c_out.b()
    grad_parts(strow[...], qg_rows, 0)
    ex_gq.start()

    def correct(t):
        ex_in.wait()
        own = innr[ia]
        for k in range(1, NI):
            own = own + rin[k]
        parts = []
        for j in range(NZ):
            coef = column(j * NI + ia) * to_col(own[j]) / D
            parts.append(t[:, j] - s2[:, j].astype(F32) * coef[None])
        return jnp.stack(parts, axis=1)

    c_norm.b(correct)
    c_out.c()
    lg.d()
    settle()
    c_norm.c()
    up = up_ref[...].astype(F32)
    branch = c_out.d()
    mixed_ref[...] = (st_ref[...].astype(F32) + gate * branch).astype(BF)
    gg_p[...] = jnp.sum(up * branch * (1.0 - gate * gate), axis=0, keepdims=True)
    ex_gi.start()
    settle()
    lg.e()
    total = jnp.zeros((NL, 128), F32)
    for h in range(HL):
        cols = slice(h * HS, (h + 1) * HS)
        total = total + dot(lg.head(h), wk_ref[:, cols], 1, 1) + dot(lg.head(HL + h), wv_ref[:, cols], 1, 1)
    rowi = lax.broadcasted_iota(jnp.int32, (NL, NL), 0)
    coli = lax.broadcasted_iota(jnp.int32, (NL, NL), 1)
    from_row = ((rowi // LR) % NJ) * LI + (rowi // (LR * NJ)) * LR + rowi % LR
    perm = (coli == from_row).astype(F32).astype(BF)
    gl[...] = dot(perm, total.astype(BF), 1, 0).astype(BF).reshape(NI, NJ * LR, 128)
    ex_gl.start()
    for h in range(HL):
        cols = slice(h * HS, (h + 1) * HS)
        gwk_ref[:, cols] = dot(latt[...], lg.head(h), 1, 0).astype(BF)
        gwv_ref[:, cols] = dot(latt[...], lg.head(HL + h), 1, 0).astype(BF)
    ex_gi.wait()
    t = gg_p[...]
    for k in range(1, NI):
        t = t + gg_r[k]
    ggj[...] = t
    ex_gj.start()
    settle()
    ex_gl.wait()
    t = gl[ia].astype(F32)
    for k in range(1, NI):
        t = t + glr[k].astype(F32)
    wide_r = lax.broadcasted_iota(jnp.int32, (NJ * 16, NJ * LR), 0)
    wide_c = lax.broadcasted_iota(jnp.int32, (NJ * 16, NJ * LR), 1)
    wide = ((wide_r // 16 * LR + wide_r % 16 == wide_c) & (wide_r % 16 < LR)).astype(F32).astype(BF)
    gls[...] = dot(wide, t.astype(BF), 1, 0).astype(BF).reshape(NJ, 16, 128)
    glf[ja] = gls[ja]
    ex_g2.start()
    gst_ref[...] = (up + c_norm.d()).astype(BF)
    settle()
    ex_go.wait()
    gwo_ref[...] = grad_sum(1).astype(BF)
    ex_gq.wait()
    gwq_ref[...] = grad_sum(0).astype(BF)
    ex_gj.wait()
    t = ggj[...]
    for k in range(1, NJ):
        t = t + ggj_r[k]
    gg_ref[...] = t
    ex_g2.wait()
    for s in range(NJ):
        glat_ref[:, s * 128 : (s + 1) * 128] = glf[s, 0:LR, :]
    for f in drains:
        f()


def finish(*refs):
    for i in range(8):
        v = refs[i][...].astype(refs[8 + i].dtype)
        refs[8 + i][...] = v.T if i == 6 else v


def run(sizes, *args):
    NI, NJ, NZ, NX = sizes
    st, lat, wq, wk, wv, wo, gate, img, cnt, up = args
    NA, NR = NZ * NX, NZ * NJ
    TB, DL = st.shape
    WB, WD = wq.shape
    HL = WD // HS
    LR = lat.shape[0]
    LI = NI * LR
    NL = NJ * LI
    LB = NL // NA
    CB = 2 * HL
    TG, DG = NR * TB, NX * WB
    assert CB == NJ and NI == NJ and NZ == 2 and NJ == NZ * NX and DL == NJ * 128 and WB == 128 and TB <= 128
    vm = lambda dt, *s: pltpu.VMEM(s, dt)

    def spread():
        return [
            vm(BF, NJ, TB, WB), vm(BF, NX, NZ, TB, WB), vm(BF, NX, NZ, TB, WB), vm(BF, NI, NX, NZ, TB, WB), vm(BF, TG, DG),
        ]

    def allsum():
        return [
            vm(BF, NX, NZ, CB, LB, 128), vm(BF, NX, NZ, CB, LB, 128), vm(BF, NZ, CB, LB, 128), vm(BF, NR, LB, 128),
            vm(BF, NX, NZ, CB, LB, 128),
        ]

    def ringsum():
        return [vm(BF, NR, TB, WD), vm(BF, 2, NR // 4, TB, WD), vm(BF, 2, NR // 4, TB, WD), vm(BF, TB, WD)]

    def collect():
        return [
            vm(BF, NI, NX, NZ, TB, WB), vm(BF, NI, NX, NZ, TB, WB), vm(BF, NX, NZ, TB, WB), vm(BF, NX, NZ, TB, WB),
            vm(BF, NJ, TB, WB),
        ]

    scratch = [
        vm(BF, 2, NX, WB, WD), vm(BF, NI, 16, DL), vm(BF, NJ, LI, 128), vm(BF, NJ, LI, 128), vm(BF, 128, NL),
        *spread(), *spread(), *allsum(), *allsum(), *ringsum(), *ringsum(),
        vm(F32, 1, TG), vm(F32, NR, 1, TG), vm(F32, NR, 1, 128), vm(F32, NX, NR, 1, 128),
        vm(BF, NR, TB, WD), vm(BF, NR, TB, WD), vm(F32, NJ, NZ, 1, 128), vm(F32, NI, NZ, 1, 128),
        *collect(), *collect(),
        vm(F32, 1, DL), vm(F32, NI, 1, DL), vm(F32, 1, DL), vm(F32, NJ, 1, DL),
        vm(BF, 2, NX, WB, WD), vm(BF, 2, NX, WB, WD),
        vm(BF, NI, NJ * LR, 128), vm(BF, NI, NJ * LR, 128), vm(BF, NJ, 16, 128), vm(BF, NJ, 16, 128),
        vm(F32, HL, TB, NL), vm(BF, HL, TB, NL),
        pltpu.SemaphoreType.DMA((420,)), pltpu.SemaphoreType.DMA((420,)),
    ]
    v, s = pl.BlockSpec(memory_space=pltpu.VMEM), pl.BlockSpec(memory_space=pltpu.SMEM)
    shape = jax.ShapeDtypeStruct
    out = pl.pallas_call(
        functools.partial(kernel, sizes),
        out_shape=(
            shape((TB, DL), BF), shape((TB, DL), BF), shape((LR, DL), BF), shape((WB, WD), BF),
            shape((WB, WD), BF), shape((WB, WD), BF), shape((WB, WD), BF), shape((1, DL), F32),
        ),
        in_specs=[v] * 8 + [s, v],
        out_specs=tuple([v] * 8),
        scratch_shapes=scratch,
        compiler_params=pltpu.CompilerParams(collective_id=0, has_side_effects=True, vmem_limit_bytes=56 * 2**20),
    )(st, lat, wq, wk, wv, wo, gate.reshape(1, DL), img.reshape(1, TB), cnt, up)
    out = pl.pallas_call(
        finish,
        out_shape=(
            shape((TB, DL), BF), shape((TB, DL), BF), shape((LR, DL), BF), shape((WB, WD), F32),
            shape((WB, WD), F32), shape((WB, WD), F32), shape((WD, WB), F32), shape((1, DL), F32),
        ),
        in_specs=[v] * 8,
        out_specs=tuple([v] * 8),
    )(*out)
    return (*out[:7], out[7].reshape(DL))


def solution(mesh, sizes=None):
    if sizes is None:
        sizes = (mesh.shape["ia"], mesh.shape["ja"], 2, mesh.shape["al"] // 2)
    tokens = P(("ja", "ia"), "al")
    weight = P(("al", "ja"), "ia")
    second = P("ia", ("al", "ja"))
    return jax.shard_map(
        functools.partial(run, sizes),
        mesh=mesh,
        in_specs=(tokens, tokens, weight, weight, weight, second, P("al"), P(("ja", "al")), P(), tokens),
        out_specs=(tokens, tokens, tokens, weight, weight, weight, second, P("al")),
        check_vma=False,
    )
```

```python
import functools
import math

import jax
import jax.numpy as jnp
from jax import lax
from jax.experimental import pallas as pl
from jax.experimental.pallas import tpu as pltpu
from jax.sharding import PartitionSpec as P

MESH = pl.DeviceIdType.MESH
D = 8192
EPS = 1e-05
BF = jnp.bfloat16
F32 = jnp.float32
IMGS = 4
HS = 128


def dot(a, b, ca, cb):
    return lax.dot_general(a, b, (((ca,), (cb,)), ((), ())), preferred_element_type=F32)


def loop(lo, hi, f):
    lax.fori_loop(lo, hi, lambda i, c: (f(i), c)[1], 0)


def kernel(sizes, *refs):
    NI, NJ, NZ, NX = sizes
    (
        st_ref, lat_ref, wq_ref, wk_ref, wv_ref, wo_ref, gate_ref, img_ref, cnt_ref, up_ref,
        mixed_ref, gst_ref, glat_ref, gwq_ref, gwk_ref, gwv_ref, gwo_ref, gg_ref,
    ) = refs[:18]
    (
        W, latg, latc, latb, latt,
        s0, s1, s2, s3, strow,
        b0, b1, b2, b3, brrow,
        kv_p, kv_rx, kv_zs, kv_rz, kv_full,
        lg_p, lg_rx, lg_zs, lg_rz, lg_full,
        q_p, q_rr, q_rl, qs,
        a_p, a_rr, a_rl, gs,
        e_p, e_r, im_z, im_x,
        atrow, qgrow, innr, rin,
        outp, outr, out1, out2, out3,
        normp, normr, norm1, norm2, norm3,
        gg_p, gg_r, ggj, ggj_r,
        gp, gpr,
        gl, glr, gls, glf,
        prob, probl,
        ssem, rsem,
    ) = refs[18:]
    NA, NR = NZ * NX, NZ * NJ
    TB, DL = st_ref.shape
    WB, WD = wq_ref.shape
    HL = WD // HS
    LR = lat_ref.shape[0]
    LI = NI * LR
    NL = NJ * LI
    LB = NL // NA
    LAT = NL // IMGS
    CB = 2 * HL
    TG = NR * TB
    DG = NX * WB
    scale = 1.0 / math.sqrt(HS)

    ia, ja, al = lax.axis_index("ia"), lax.axis_index("ja"), lax.axis_index("al")
    x, zh = lax.rem(al, NX), lax.div(al, NX)
    z = zh * NJ + ja
    place = {"ia": (ia, NI), "ja": (ja, NJ), "x": (x, NX), "z": (z, NR)}

    def device(axis, i):
        if axis == "x":
            return {"al": zh * NX + i}
        if axis == "z":
            return {"ja": lax.rem(i, NJ), "al": lax.div(i, NJ) * NX + x}
        return {axis: i}

    used = [0]
    drains = []
    seen = [0]

    def settle():
        for f in drains[: seen[0]]:
            f()
        del drains[: seen[0]]
        seen[0] = len(drains)


    def take(n):
        used[0] += n
        assert used[0] <= ssem.shape[0]
        return used[0] - n

    def copy(src, dst, i, dev):
        return pltpu.make_async_remote_copy(
            src_ref=src, dst_ref=dst, send_sem=ssem.at[i], recv_sem=rsem.at[i],
            device_id=dev, device_id_type=MESH,
        )

    class Exchange:
        def __init__(self, axis, src, dst):
            self.axis, self.src, self.dst = axis, src, dst
            self.me, self.n = place[axis]
            self.base = take(self.n)

        def out(self, k):
            peer = lax.rem(self.me + k, self.n)
            return copy(self.src(peer), self.dst(self.me, k), self.base + k, device(self.axis, peer))

        def into(self, k):
            peer = lax.rem(self.me - k + self.n, self.n)
            return copy(self.src(peer), self.dst(peer, k), self.base + k, device(self.axis, peer))

        def start(self):
            loop(1, self.n, lambda k: self.out(k).start())
            drains.append(lambda: loop(1, self.n, lambda k: self.out(k).wait_send()))

        def wait(self):
            loop(1, self.n, lambda k: self.into(k).wait_recv())

    HOPS = NR // 4
    ring = {d: device("z", lax.rem(z + d + NR, NR)) for d in (-2, -1, 1, 2)}

    class RingSum:
        def __init__(self, p, odd, even):
            self.p, self.odd, self.even = p, odd, even
            self.o = {g: take(HOPS) for g in (1, -1)}
            self.e = {g: take(HOPS) for g in (1, -1)}

        def block(self, g, off):
            return self.p.at[lax.rem(z + g * off + NR, NR)]

        def one(self, g, i, src=None):
            dst = self.odd.at[(1 - g) // 2, i]
            return copy(dst if src is None else src, dst, self.o[g] + i, ring[g])

        def two(self, g, s, src=None):
            dst = self.even.at[(1 - g) // 2, s]
            return copy(dst if src is None else src, dst, self.e[g] + s, ring[2 * g])

        def source(self, g, s):
            if s == 0:
                return self.block(1, 2 * HOPS)
            return self.odd.at[1, 0] if g < 0 and s == 1 else self.even.at[(1 - g) // 2, s - 1]

        def step(self, s):
            if s == 0:
                self.two(1, 0, self.source(1, 0)).start()
                for i in range(HOPS):
                    for g in (1, -1):
                        self.one(g, i, self.block(g, 2 * HOPS - 1 - 2 * i)).start()
                return
            for g in (1, -1):
                self.one(g, s - 1).wait_recv()
                t = self.odd[(1 - g) // 2, s - 1].astype(F32) + self.block(g, 2 * HOPS - 2 * s)[...].astype(F32)
                if g > 0 or s > 1:
                    self.two(g, s - 1).wait_recv()
                    t = t + self.even[(1 - g) // 2, s - 1].astype(F32)
                src = self.source(g, s)
                src[...] = t.astype(BF)
                self.two(g, s, src).start()

        def end(self):
            t = self.p[z].astype(F32)
            for g in (1, -1):
                self.one(g, HOPS - 1).wait_recv()
                self.two(g, HOPS - 1).wait_recv()
                t = t + self.odd[(1 - g) // 2, HOPS - 1].astype(F32) + self.even[(1 - g) // 2, HOPS - 1].astype(F32)

            def drain():
                for s in range(HOPS):
                    for g in (1, -1):
                        self.one(g, s).wait_send()
                        if g > 0 or s > 0:
                            self.two(g, s).wait_send()

            drains.append(drain)
            return t

    class RingGather:
        def __init__(self, buf):
            self.buf = buf
            self.o = {g: take(HOPS) for g in (1, -1)}
            self.e = {g: take(HOPS) for g in (1, -1)}

        def one(self, g, s, frm):
            b = self.buf.at[lax.rem(z - g * frm + NR, NR)]
            return copy(b, b, self.o[g] + s, ring[g])

        def two(self, g, s, frm):
            b = self.buf.at[lax.rem(z - g * frm + NR, NR)]
            return copy(b, b, self.e[g] + s, ring[2 * g])

        def step(self, s):
            for g in (1, -1):
                if s > 0:
                    self.two(g, s - 1, 2 * s).wait_recv()
                if g > 0 or s < HOPS - 1:
                    self.two(g, s, 2 * s).start()
                self.one(g, s, 2 * s).start()

        def end(self):
            self.two(1, HOPS - 1, 2 * HOPS).wait_recv()
            for g in (1, -1):
                for s in range(HOPS):
                    self.one(g, s, 2 * s + 1).wait_recv()

            def drain():
                for g in (1, -1):
                    for s in range(HOPS):
                        self.one(g, s, 2 * s).wait_send()
                        if g > 0 or s < HOPS - 1:
                            self.two(g, s, 2 * s).wait_send()

            drains.append(drain)

    class AllSum:
        def __init__(self, p, rx, zs, rz, full):
            self.p, self.rx, self.zs, self.rz, self.full = p, rx, zs, rz, full
            self.x1 = Exchange("x", lambda peer: p.at[peer], lambda s, k: rx.at[k])
            self.z1 = Exchange("z", lambda peer: zs.at[lax.div(peer, NJ), lax.rem(peer, NJ)], lambda s, k: rz.at[k])
            self.z2 = Exchange("z", lambda peer: full.at[x, zh, ja], lambda s, k: full.at[x, lax.div(s, NJ), lax.rem(s, NJ)])
            self.x2 = Exchange("x", lambda peer: full.at[x], lambda s, k: full.at[s])

        def a(self):
            self.x1.start()

        def b(self):
            self.x1.wait()
            t = self.p[x].astype(F32)
            for k in range(1, NX):
                t = t + self.rx[k].astype(F32)
            self.zs[...] = t.astype(BF)
            self.z1.start()

        def c(self):
            self.z1.wait()
            t = self.zs[zh, ja].astype(F32)
            for k in range(1, NR):
                t = t + self.rz[k].astype(F32)
            self.full[x, zh, ja] = t.astype(BF)
            self.z2.start()

        def d(self):
            self.z2.wait()
            self.x2.start()

        def e(self):
            self.x2.wait()

        def head(self, h):
            return jnp.concatenate([self.full[a % NX, a // NX, h] for a in range(NA)], axis=0)

    class Spread:
        def __init__(self, t0, t1, t2, t3, rows):
            self.t0, self.t1, self.t2, self.t3, self.rows = t0, t1, t2, t3, rows
            self.z = Exchange("ja", lambda peer: t0.at[peer], lambda s, k: t1.at[lax.div(s, NZ), lax.rem(s, NZ)])
            self.x = Exchange("x", lambda peer: t1.at[peer], lambda s, k: t2.at[s])
            self.y = Exchange("ia", lambda peer: t3.at[ia], lambda s, k: t3.at[s])

        def load(self, v):
            for s in range(NJ):
                self.t0[s] = v[:, s * WB : (s + 1) * WB]
            self.t1[ja // NZ, ja % NZ] = self.t0[ja]

        def a(self):
            self.z.start()

        def b(self):
            self.z.wait()
            self.x.start()

        def c(self):
            self.x.wait()
            self.t2[x] = self.t1[x]
            self.t3[ia] = self.t2[...]
            self.y.start()

        def d(self):
            self.y.wait()
            for k in range(NX):
                for j in range(NZ):
                    self.rows[j * NI * TB : (j + 1) * NI * TB, k * WB : (k + 1) * WB] = self.t3[:, k, j].reshape(NI * TB, WB)

    class Collect:
        def __init__(self, p, r, t1, t2, t3):
            self.p, self.r, self.t1, self.t2, self.t3 = p, r, t1, t2, t3
            self.y = Exchange("ia", lambda peer: p.at[peer], lambda s, k: r.at[k])
            self.x = Exchange("x", lambda peer: t1.at[peer], lambda s, k: t2.at[s])
            self.z = Exchange("ja", lambda peer: t2.at[lax.div(peer, NZ), lax.rem(peer, NZ)], lambda s, k: t3.at[s])

        def a(self, rows, m):
            for k in range(NX):
                v = dot(rows, W[m, k], 1, 1).astype(BF)
                for j in range(NZ):
                    self.p[:, k, j] = v[j * NI * TB : (j + 1) * NI * TB].reshape(NI, TB, WB)
            self.y.start()

        def b(self, correct=None):
            self.y.wait()
            t = self.p[ia].astype(F32)
            for k in range(1, NI):
                t = t + self.r[k].astype(F32)
            if correct is not None:
                t = correct(t)
            self.t1[...] = t.astype(BF)
            self.t2[x] = self.t1[x]
            self.x.start()

        def c(self):
            self.x.wait()
            self.t3[ja] = self.t2[ja // NZ, ja % NZ]
            self.z.start()

        def d(self):
            self.z.wait()
            return jnp.concatenate([self.t3[s] for s in range(NJ)], axis=1).astype(F32)

    ex_wq = Exchange("x", lambda peer: W.at[0, x], lambda s, k: W.at[0, s])
    ex_wo = Exchange("x", lambda peer: W.at[1, x], lambda s, k: W.at[1, s])
    ex_lat = Exchange("ia", lambda peer: latg.at[ia], lambda s, k: latg.at[s])
    ex_l2 = Exchange("ja", lambda peer: latc.at[peer], lambda s, k: latb.at[s])
    sp_s, sp_b = Spread(s0, s1, s2, s3, strow), Spread(b0, b1, b2, b3, brrow)
    kv = AllSum(kv_p, kv_rx, kv_zs, kv_rz, kv_full)
    lg = AllSum(lg_p, lg_rx, lg_zs, lg_rz, lg_full)
    q_s, a_s = RingSum(q_p, q_rr, q_rl), RingSum(a_p, a_rr, a_rl)
    e_z = Exchange("z", lambda peer: e_p, lambda s, k: e_r.at[k])
    ex_iz = Exchange("z", lambda peer: im_z.at[z], lambda s, k: im_z.at[s])
    ex_ix = Exchange("x", lambda peer: im_x.at[x], lambda s, k: im_x.at[s])
    at_g, qg_g = RingGather(atrow), RingGather(qgrow)
    in_g = Exchange("z", lambda peer: innr.at[ja, zh], lambda s, k: innr.at[lax.rem(s, NJ), lax.div(s, NJ)])
    ex_in = Exchange("ia", lambda peer: innr.at[peer], lambda s, k: rin.at[k])
    c_out, c_norm = Collect(outp, outr, out1, out2, out3), Collect(normp, normr, norm1, norm2, norm3)
    ex_gi = Exchange("ia", lambda peer: gg_p, lambda s, k: gg_r.at[k])
    ex_gj = Exchange("ja", lambda peer: ggj, lambda s, k: ggj_r.at[k])
    ex_gq = Exchange("x", lambda peer: gp.at[0, peer], lambda s, k: gpr.at[0, k])
    ex_go = Exchange("x", lambda peer: gp.at[1, peer], lambda s, k: gpr.at[1, k])
    ex_gl = Exchange("ia", lambda peer: gl.at[peer], lambda s, k: glr.at[k])
    ex_g2 = Exchange("ja", lambda peer: gls.at[peer], lambda s, k: glf.at[s])

    barrier = pltpu.get_barrier_semaphore()
    for axis in ("ia", "x", "z"):
        i, n = place[axis]
        loop(1, n, lambda k: pl.semaphore_signal(barrier, 1, device_id=device(axis, lax.rem(i + k, n)), device_id_type=MESH))

    lane1 = lax.broadcasted_iota(jnp.int32, (TB, 128), 1)
    sub1 = lax.broadcasted_iota(jnp.int32, (TB, 128), 0)

    def to_row(col):
        return jnp.sum(jnp.where(lane1 == sub1, col, 0.0), axis=0, keepdims=True)

    def to_col(row):
        return jnp.sum(jnp.where(lane1 == sub1, row, 0.0), axis=1, keepdims=True)

    sp_s.load(st_ref[...])
    latg[ia] = jnp.zeros((16, DL), BF)
    latg[ia, 0:LR, :] = lat_ref[...]
    W[0, x] = wq_ref[...]
    gate = jnp.tanh(gate_ref[...])
    sp_b.load((up_ref[...].astype(F32) * gate).astype(BF))
    im_z[z] = jnp.zeros((1, 128), F32)
    im_z[z, :, 0:TB] = img_ref[...].astype(F32)
    pl.semaphore_wait(barrier, NI - 1 + NX - 1 + NR - 1)

    sp_s.a()
    ex_lat.start()
    sp_b.a()
    W[1, x] = wo_ref[...].T

    sp_s.b()
    ex_wq.start()
    ex_iz.start()
    ex_lat.wait()
    pick_r = lax.broadcasted_iota(jnp.int32, (LI, NI * 16), 0)
    pick_c = lax.broadcasted_iota(jnp.int32, (LI, NI * 16), 1)
    pick = (pick_c == (pick_r // LR) * 16 + pick_r % LR).astype(F32).astype(BF)
    packed = dot(pick, latg[...].reshape(NI * 16, DL), 1, 0).astype(BF)
    for s in range(NJ):
        latc[s] = packed[:, s * 128 : (s + 1) * 128]
    latb[ja] = latc[ja]
    ex_l2.start()
    sp_s.c()
    sp_b.b()
    ex_iz.wait()
    im_x[x] = im_z[...]
    ex_ix.start()

    settle()
    ex_l2.wait()
    lat = latb[...].reshape(NL, 128)
    latt[...] = lat.T
    for h in range(CB):
        wref = wk_ref if h < HL else wv_ref
        c = h % HL
        part = dot(lat, wref[:, c * HS : (c + 1) * HS], 1, 0).astype(BF)
        for a in range(NA):
            kv_p[a % NX, a // NX, h] = part[a * LB : (a + 1) * LB]
    sp_b.c()
    kv.a()
    ex_wo.start()

    def rows_times(rows, m, p):
        acc = dot(rows, W[m].reshape(DG, WD), 1, 0).astype(BF)
        for d in range(NR):
            p[d] = acc[d * TB : (d + 1) * TB]

    settle()
    sp_s.d()
    ex_wq.wait()
    rows_times(strow[...], 0, q_p)
    q_s.step(0)
    sq = strow[...].astype(F32)
    sq = (sq * sq).astype(BF)
    e_p[...] = dot(jnp.ones((8, DG), BF), sq, 1, 1)[0:1]
    e_z.start()
    kv.b()
    settle()
    sp_b.d()
    ex_wo.wait()
    rows_times(brrow[...], 1, a_p)
    a_s.step(0)
    q_s.step(1)
    a_s.step(1)
    kv.c()
    for s in range(2, HOPS):
        settle()
        q_s.step(s)
        a_s.step(s)
    kv.d()
    e_z.wait()
    energy = e_p[...]
    for k in range(1, NR):
        energy = energy + e_r[k]
    inv_row = lax.rsqrt(energy / D + EPS)
    lane = lax.broadcasted_iota(jnp.int32, (TB, TG), 1)
    sub = lax.broadcasted_iota(jnp.int32, (TB, TG), 0)

    def column(block):
        return jnp.sum(jnp.where(lane == block * TB + sub, inv_row, 0.0), axis=1, keepdims=True)

    inv_attn = column(z)
    ex_ix.wait()
    image_col = to_col(im_x[ja % NX, (ja // NX) * NJ + NZ * x + zh])
    slot = lax.broadcasted_iota(jnp.int32, (TB, NL), 1)
    image = slot // LAT
    count = jnp.where(image == 0, cnt_ref[0], jnp.where(image == 1, cnt_ref[1], jnp.where(image == 2, cnt_ref[2], cnt_ref[3])))
    allowed = (image_col == image.astype(F32)) & (slot % LAT < count)
    q = q_s.end() * inv_attn
    qs[...] = q.astype(BF)
    gs[...] = a_s.end().astype(BF)
    settle()
    kv.e()
    for h in range(HL):
        cols = slice(h * HS, (h + 1) * HS)
        sco = dot(qs[:, cols], kv.head(h), 1, 1) * scale
        raised = jnp.where(allowed, jnp.exp(sco), 0.0)
        pr = raised / jnp.sum(raised, axis=1, keepdims=True)
        prob[h] = pr
        probl[h] = pr.astype(BF)
        atrow[z, :, cols] = dot(probl[h], kv.head(HL + h), 1, 0).astype(BF)
    at_g.step(0)
    inner = jnp.zeros((TB, 1), F32)
    for h in range(HL):
        cols = slice(h * HS, (h + 1) * HS)
        kh = kv.head(h)
        gh = gs[:, cols]
        qh = qs[:, cols]
        pg = dot(gh, kv.head(HL + h), 1, 1)
        pr = prob[h]
        sg = pr * (pg - jnp.sum(pr * pg, axis=1, keepdims=True))
        sl = sg.astype(BF)
        qg = dot(sl, kh, 1, 0) * scale * inv_attn
        inner = inner + jnp.sum(qg * qh.astype(F32), axis=1, keepdims=True)
        qgrow[z, :, cols] = qg.astype(BF)
        kt = (dot(sl, qh, 0, 0) * scale).astype(BF)
        vt = dot(probl[h], gh, 0, 0).astype(BF)
        for a in range(NA):
            lg_p[a % NX, a // NX, h] = kt[a * LB : (a + 1) * LB]
            lg_p[a % NX, a // NX, HL + h] = vt[a * LB : (a + 1) * LB]
    qg_g.step(0)
    lg.a()
    innr[ja, zh] = to_row(inner)
    in_g.start()
    at_g.step(1)
    qg_g.step(1)
    lg.b()
    for s in range(2, HOPS):
        settle()
        at_g.step(s)
        qg_g.step(s)

    def grad_parts(left_rows, right_rows, m):
        for k in range(NX):
            gp[m, k] = dot(left_rows[:, k * WB : (k + 1) * WB], right_rows, 0, 0).astype(BF)

    def grad_sum(m):
        t = gp[m, x].astype(F32)
        for k in range(1, NX):
            t = t + gpr[m, k].astype(F32)
        return t

    at_g.end()
    attn_rows = atrow[...].reshape(TG, WD)
    c_out.a(attn_rows, 1)
    qg_g.end()
    qg_rows = qgrow[...].reshape(TG, WD)
    c_norm.a(qg_rows, 0)
    lg.c()
    in_g.wait()
    ex_in.start()
    grad_parts(brrow[...], attn_rows, 1)
    ex_go.start()
    settle()
    c_out.b()
    grad_parts(strow[...], qg_rows, 0)
    ex_gq.start()

    def correct(t):
        ex_in.wait()
        own = innr[ia]
        for k in range(1, NI):
            own = own + rin[k]
        parts = []
        for j in range(NZ):
            coef = column(j * NI + ia) * to_col(own[j]) / D
            parts.append(t[:, j] - s2[:, j].astype(F32) * coef[None])
        return jnp.stack(parts, axis=1)

    c_norm.b(correct)
    c_out.c()
    lg.d()
    settle()
    c_norm.c()
    up = up_ref[...].astype(F32)
    branch = c_out.d()
    mixed_ref[...] = (st_ref[...].astype(F32) + gate * branch).astype(BF)
    gg_p[...] = jnp.sum(up * branch * (1.0 - gate * gate), axis=0, keepdims=True)
    ex_gi.start()
    settle()
    lg.e()
    total = jnp.zeros((NL, 128), F32)
    for h in range(HL):
        cols = slice(h * HS, (h + 1) * HS)
        total = total + dot(lg.head(h), wk_ref[:, cols], 1, 1) + dot(lg.head(HL + h), wv_ref[:, cols], 1, 1)
    rowi = lax.broadcasted_iota(jnp.int32, (NL, NL), 0)
    coli = lax.broadcasted_iota(jnp.int32, (NL, NL), 1)
    from_row = ((rowi // LR) % NJ) * LI + (rowi // (LR * NJ)) * LR + rowi % LR
    perm = (coli == from_row).astype(F32).astype(BF)
    gl[...] = dot(perm, total.astype(BF), 1, 0).astype(BF).reshape(NI, NJ * LR, 128)
    ex_gl.start()
    for h in range(HL):
        cols = slice(h * HS, (h + 1) * HS)
        gwk_ref[:, cols] = dot(latt[...], lg.head(h), 1, 0).astype(BF)
        gwv_ref[:, cols] = dot(latt[...], lg.head(HL + h), 1, 0).astype(BF)
    ex_gi.wait()
    t = gg_p[...]
    for k in range(1, NI):
        t = t + gg_r[k]
    ggj[...] = t
    ex_gj.start()
    settle()
    ex_gl.wait()
    t = gl[ia].astype(F32)
    for k in range(1, NI):
        t = t + glr[k].astype(F32)
    wide_r = lax.broadcasted_iota(jnp.int32, (NJ * 16, NJ * LR), 0)
    wide_c = lax.broadcasted_iota(jnp.int32, (NJ * 16, NJ * LR), 1)
    wide = ((wide_r // 16 * LR + wide_r % 16 == wide_c) & (wide_r % 16 < LR)).astype(F32).astype(BF)
    gls[...] = dot(wide, t.astype(BF), 1, 0).astype(BF).reshape(NJ, 16, 128)
    glf[ja] = gls[ja]
    ex_g2.start()
    gst_ref[...] = (up + c_norm.d()).astype(BF)
    settle()
    ex_go.wait()
    gwo_ref[...] = grad_sum(1).astype(BF)
    ex_gq.wait()
    gwq_ref[...] = grad_sum(0).astype(BF)
    ex_gj.wait()
    t = ggj[...]
    for k in range(1, NJ):
        t = t + ggj_r[k]
    gg_ref[...] = t
    ex_g2.wait()
    for s in range(NJ):
        glat_ref[:, s * 128 : (s + 1) * 128] = glf[s, 0:LR, :]
    for f in drains:
        f()


def finish(*refs):
    for i in range(8):
        v = refs[i][...].astype(refs[8 + i].dtype)
        refs[8 + i][...] = v.T if i == 6 else v


def run(sizes, *args):
    NI, NJ, NZ, NX = sizes
    st, lat, wq, wk, wv, wo, gate, img, cnt, up = args
    NA, NR = NZ * NX, NZ * NJ
    TB, DL = st.shape
    WB, WD = wq.shape
    HL = WD // HS
    LR = lat.shape[0]
    LI = NI * LR
    NL = NJ * LI
    LB = NL // NA
    CB = 2 * HL
    TG, DG = NR * TB, NX * WB
    assert CB == NJ and NI == NJ and NZ == 2 and NJ == NZ * NX and DL == NJ * 128 and WB == 128 and TB <= 128
    vm = lambda dt, *s: pltpu.VMEM(s, dt)

    def spread():
        return [
            vm(BF, NJ, TB, WB), vm(BF, NX, NZ, TB, WB), vm(BF, NX, NZ, TB, WB), vm(BF, NI, NX, NZ, TB, WB), vm(BF, TG, DG),
        ]

    def allsum():
        return [
            vm(BF, NX, NZ, CB, LB, 128), vm(BF, NX, NZ, CB, LB, 128), vm(BF, NZ, CB, LB, 128), vm(BF, NR, LB, 128),
            vm(BF, NX, NZ, CB, LB, 128),
        ]

    def ringsum():
        return [vm(BF, NR, TB, WD), vm(BF, 2, NR // 4, TB, WD), vm(BF, 2, NR // 4, TB, WD), vm(BF, TB, WD)]

    def collect():
        return [
            vm(BF, NI, NX, NZ, TB, WB), vm(BF, NI, NX, NZ, TB, WB), vm(BF, NX, NZ, TB, WB), vm(BF, NX, NZ, TB, WB),
            vm(BF, NJ, TB, WB),
        ]

    scratch = [
        vm(BF, 2, NX, WB, WD), vm(BF, NI, 16, DL), vm(BF, NJ, LI, 128), vm(BF, NJ, LI, 128), vm(BF, 128, NL),
        *spread(), *spread(), *allsum(), *allsum(), *ringsum(), *ringsum(),
        vm(F32, 1, TG), vm(F32, NR, 1, TG), vm(F32, NR, 1, 128), vm(F32, NX, NR, 1, 128),
        vm(BF, NR, TB, WD), vm(BF, NR, TB, WD), vm(F32, NJ, NZ, 1, 128), vm(F32, NI, NZ, 1, 128),
        *collect(), *collect(),
        vm(F32, 1, DL), vm(F32, NI, 1, DL), vm(F32, 1, DL), vm(F32, NJ, 1, DL),
        vm(BF, 2, NX, WB, WD), vm(BF, 2, NX, WB, WD),
        vm(BF, NI, NJ * LR, 128), vm(BF, NI, NJ * LR, 128), vm(BF, NJ, 16, 128), vm(BF, NJ, 16, 128),
        vm(F32, HL, TB, NL), vm(BF, HL, TB, NL),
        pltpu.SemaphoreType.DMA((420,)), pltpu.SemaphoreType.DMA((420,)),
    ]
    v, s = pl.BlockSpec(memory_space=pltpu.VMEM), pl.BlockSpec(memory_space=pltpu.SMEM)
    shape = jax.ShapeDtypeStruct
    out = pl.pallas_call(
        functools.partial(kernel, sizes),
        out_shape=(
            shape((TB, DL), BF), shape((TB, DL), BF), shape((LR, DL), BF), shape((WB, WD), BF),
            shape((WB, WD), BF), shape((WB, WD), BF), shape((WB, WD), BF), shape((1, DL), F32),
        ),
        in_specs=[v] * 8 + [s, v],
        out_specs=tuple([v] * 8),
        scratch_shapes=scratch,
        compiler_params=pltpu.CompilerParams(collective_id=0, has_side_effects=True, vmem_limit_bytes=56 * 2**20),
    )(st, lat, wq, wk, wv, wo, gate.reshape(1, DL), img.reshape(1, TB), cnt, up)
    out = pl.pallas_call(
        finish,
        out_shape=(
            shape((TB, DL), BF), shape((TB, DL), BF), shape((LR, DL), BF), shape((WB, WD), F32),
            shape((WB, WD), F32), shape((WB, WD), F32), shape((WD, WB), F32), shape((1, DL), F32),
        ),
        in_specs=[v] * 8,
        out_specs=tuple([v] * 8),
    )(*out)
    return (*out[:7], out[7].reshape(DL))


def solution(mesh, sizes=None):
    if sizes is None:
        sizes = (mesh.shape["ia"], mesh.shape["ja"], 2, mesh.shape["al"] // 2)
    tokens = P(("ja", "ia"), "al")
    weight = P(("al", "ja"), "ia")
    second = P("ia", ("al", "ja"))
    return jax.shard_map(
        functools.partial(run, sizes),
        mesh=mesh,
        in_specs=(tokens, tokens, weight, weight, weight, second, P("al"), P(("ja", "al")), P(), tokens),
        out_specs=(tokens, tokens, tokens, weight, weight, weight, second, P("al")),
        check_vma=False,
    )
```
